32 devices in a mesh: image: 4 (over y, x), token: 8 (over z, core).
Axes of the slice: x: 2, y: 2, z: 4, core: 2. Of those that a mesh axis runs over, the one named last changes fastest.
Arguments:
- hidden: bfloat16 [2, 4, 1024, 3072], P(None, 'image', 'token'), may hold values from -6 to 6
- key_cache: bfloat16 [2, 4, 1024, 1536], P(None, 'image', 'token')
- value_cache: bfloat16 [2, 4, 1024, 1536], P(None, 'image', 'token'), may hold values from -6 to 6
- cached_out: bfloat16 [4, 1024, 1536], P('image', 'token'), may hold values from -6 to 6
- w_query: bfloat16 [3072, 1536], P('image'), may hold values from -0.109375 to 0.109375
- guide: float32 [4], P('image'), may hold values from 1.5 to 4
- masked_tiles: int32 [4, 2], P('image'), may hold values from 0 to 7, as said below
- mask_count: int32 [4], P('image'), may hold values from 1 to 2, as said below
Outputs:
- edited: bfloat16 [4, 1024, 1536], P('image', 'token')
The draws below stay inside these ranges and needn't reach their ends.
Inputs may be any that keep to these rules, and one draw needn't show every extreme that they name: `masked_tiles`: in each image the first mask_count entries are distinct tiles; later entries are tiles too. `mask_count`: some image of every draw has exactly 2 masked tiles.
All inputs are finite; a program needn't handle non-finite values.
Results may differ from the reference program's by a relative error of at most 0.011.
The reference program's roundings to bfloat16 on the way count: a program that leaves them out, or rounds other values in their place, can miss the bound.
Values may be sent and summed in bfloat16 or wider, within the bound.
No kernel may reach another device: no remote copies, remote signals or barrier semaphores. Data moves between devices by JAX's collectives and lax.ppermute only.
A program may use at most 128 MiB of HBM per device.

```python
import math
import jax
import jax.numpy as jnp
from jax import lax

D = 3072
HD = 128
HEADS = 12
INNER = 1536
TILE = 128
L = 1024
IMAGE_COUNT = 4
MASK_MOST = 2


def mask_layout(key):
    starting_key = jax.random.fold_in(key, 17)
    image_keys = jax.random.split(jax.random.fold_in(starting_key, 1), IMAGE_COUNT)

    def one_image(image_key):
        return jax.random.permutation(image_key, L // TILE)[:MASK_MOST].astype(jnp.int32)
    tiles = jax.vmap(one_image)(image_keys).astype(jnp.int32)
    counts = jax.random.randint(jax.random.fold_in(starting_key, 2), (IMAGE_COUNT,), (MASK_MOST + 1) // 2, MASK_MOST + 1).astype(jnp.int32)
    fullest = jax.random.randint(jax.random.fold_in(starting_key, 3), (), 0, IMAGE_COUNT)
    counts = jnp.where(jnp.arange(IMAGE_COUNT) == fullest, MASK_MOST, counts).astype(jnp.int32)
    return (tiles, counts)


def draw_masked_tiles(key, part):
    tiles, counts = mask_layout(key)
    return tiles


def draw_mask_count(key, part):
    tiles, counts = mask_layout(key)
    return counts


def draw_key_cache(key, part):
    shape = (2, IMAGE_COUNT, L, HEADS * HD)
    entries = jax.random.normal(jax.random.fold_in(key, 5), shape, jnp.float32)
    return entries.astype(jnp.bfloat16)


def level_of(rng, dims, cuts, smallest, high):
    loudness, own = 1.0, jax.random.fold_in(rng, 6)
    for dim, parts in cuts:
        heights = jnp.exp(jax.random.uniform(jax.random.fold_in(own, dim), (parts,), jnp.float32, smallest / len(cuts), high / len(cuts)))
        loudness = loudness * jnp.repeat(heights, dims[dim] // parts).reshape([-1 if axis == dim else 1 for axis in range(len(dims))])
    return loudness


def scatter_about(own_key, shape, scale, reach, pieces=(), held_as=jnp.bfloat16):
    level = level_of(own_key, shape, pieces, -0.22, 0.18) if pieces else 1.0
    array = jax.random.normal(own_key, shape, jnp.float32) * scale * level
    return jnp.minimum(jnp.maximum(array, -reach), reach).astype(held_as)


def setup_inputs(seed: int = 0) -> dict:
    key_of = jax.random.split(jax.random.key(seed), 9)
    return {
        "hidden": scatter_about(key_of[0], (2, IMAGE_COUNT, L, D), 1.0, 6.0, ((1, 4), (2, 8))),
        "key_cache": draw_key_cache(jax.random.fold_in(key_of[8], 71), 0),
        "value_cache": scatter_about(key_of[2], (2, IMAGE_COUNT, L, INNER), 1.0, 6.0, ((1, 4), (2, 8))),
        "cached_out": scatter_about(key_of[3], (IMAGE_COUNT, L, INNER), 1.0, 6.0, ((0, 4), (1, 8))),
        "w_query": scatter_about(key_of[4], (D, INNER), D ** -0.5, 0.109375, ((0, 4),)),
        "guide": jnp.clip(1.5 + 2.5 * jax.random.uniform(key_of[5], (IMAGE_COUNT,), jnp.float32) ** level_of(key_of[5], (IMAGE_COUNT,), ((0, 4),), -0.2, 0.2), 1.5, 4.0),
        "masked_tiles": draw_masked_tiles(jax.random.fold_in(key_of[8], 71), 0),
        "mask_count": draw_mask_count(jax.random.fold_in(key_of[8], 71), 0),
    }


def one_head(operands):
    head_queries, head_keys, head_values = operands
    scale_for_scores = 1.0 / math.sqrt(HD)
    logit_scores = jnp.einsum('tzh,tjh->tzj', head_queries.astype(jnp.float32), head_keys.astype(jnp.float32), precision=lax.Precision.HIGHEST) * scale_for_scores
    row_max = lax.optimization_barrier(jnp.max(logit_scores, axis=-1, keepdims=True))
    exp_scores = jnp.exp(logit_scores - row_max)
    row_total = lax.optimization_barrier(jnp.sum(exp_scores, axis=-1, keepdims=True))
    softmax_weights = (exp_scores / row_total).astype(jnp.bfloat16)
    return jnp.einsum('enj,ejh->enh', softmax_weights.astype(jnp.float32), head_values.astype(jnp.float32), precision=lax.Precision.HIGHEST)

def attend(queries, key_block, value_block):
    rows_all = queries.shape[1]
    query_heads = jnp.moveaxis(queries.reshape(2, rows_all, HEADS, HD), 2, 0)
    key_heads = jnp.moveaxis(key_block.reshape(2, L, HEADS, HD), 2, 0)
    value_heads = jnp.moveaxis(value_block.reshape(2, L, HEADS, HD), 2, 0)
    attended = lax.map(one_head, (query_heads, key_heads, value_heads))
    return jnp.moveaxis(attended, 0, 2).reshape(2, rows_all, HEADS * HD)

def reference(hidden, key_cache, value_cache, cached_out, w_query, guide, masked_tiles, mask_count):
    edited_all = []
    for image_index in range(IMAGE_COUNT):
        image_hidden = hidden[:, image_index]
        starts = (masked_tiles[image_index] * TILE).astype(jnp.int32)

        def take_tile(first_row):
            return lax.dynamic_slice_in_dim(image_hidden, first_row, TILE, 1)
        tile_rows = jax.vmap(take_tile)(starts)
        tile_rows = jnp.moveaxis(tile_rows, 0, 1).reshape(2 * MASK_MOST * TILE, D)
        queries = jnp.dot(tile_rows, w_query, preferred_element_type=jnp.float32).astype(jnp.bfloat16)
        queries = queries.reshape(2, MASK_MOST * TILE, HEADS * HD)
        attended = attend(queries, key_cache[:, image_index], value_cache[:, image_index])
        guided = attended[1] + guide[image_index] * (attended[0] - attended[1])
        guided = guided.astype(jnp.bfloat16).reshape(MASK_MOST, TILE, HEADS * HD)
        field_out = cached_out[image_index]
        for slot_index in range(MASK_MOST):
            first_row = (masked_tiles[image_index, slot_index] * TILE).astype(jnp.int32)
            previous = lax.dynamic_slice_in_dim(field_out, first_row, TILE, 0)
            chosen = jnp.where(slot_index < mask_count[image_index], guided[slot_index], previous)
            field_out = lax.dynamic_update_slice_in_dim(field_out, chosen, first_row, 0)
        edited_all.append(field_out)
    return jnp.stack(edited_all)
```

```python
import math

import jax
import jax.numpy as jnp
from jax import lax
from jax.experimental import pallas as pl
from jax.experimental.pallas import tpu as pltpu
from jax.sharding import PartitionSpec as P

HD = 128
TILE = 128
GROUPS = 4
BF = jnp.bfloat16
F32 = jnp.float32
VMEM_LIMIT = 48 * 1024 * 1024

SMEM_SPEC = pl.BlockSpec(memory_space=pltpu.SMEM)
VMEM_SPEC = pl.BlockSpec(memory_space=pltpu.VMEM)


def call(kernel, out_shape, scalars, arrays, flops, moved, scratch=(), exps=0):
    many = isinstance(out_shape, (list, tuple))
    return pl.pallas_call(
        kernel,
        out_shape=out_shape,
        in_specs=[SMEM_SPEC] + [VMEM_SPEC] * len(arrays),
        out_specs=[VMEM_SPEC] * len(out_shape) if many else VMEM_SPEC,
        scratch_shapes=list(scratch),
        compiler_params=pltpu.CompilerParams(vmem_limit_bytes=VMEM_LIMIT),
        cost_estimate=pl.CostEstimate(flops=flops, bytes_accessed=moved, transcendentals=exps),
    )(scalars, *arrays)


def pack_weights(core, w_query, parts):
    rows, columns = w_query.shape
    half = columns // 2
    width = 2 * HD

    def kernel(core_ref, w_ref, *out_refs):
        for k, out in enumerate(out_refs):
            for hi in range(2):
                at = pl.multiple_of(core_ref[0] * half + (hi * parts + k) * HD, HD)
                out[:, hi * HD : (hi + 1) * HD] = w_ref[:, pl.ds(at, HD)]

    return call(
        kernel,
        [jax.ShapeDtypeStruct((rows, width), BF)] * parts,
        core,
        [w_query],
        0,
        2 * rows * columns * 3,
    )


def pack_keys(z_pos, key_block, value_block):
    branches, tokens, columns = key_block.shape
    width = columns // GROUPS

    def kernel(z_ref, k_ref, v_ref, *out_refs):
        for m, out in enumerate(out_refs):
            at = pl.multiple_of((z_ref[0] ^ m) * width, HD)
            out[0] = k_ref[:, :, pl.ds(at, width)]
            out[1] = v_ref[:, :, pl.ds(at, width)]

    return call(
        kernel,
        [jax.ShapeDtypeStruct((2, branches, tokens, width), BF)] * GROUPS,
        z_pos,
        [key_block, value_block],
        0,
        2 * 4 * branches * tokens * columns,
    )


def project(scalars, own, other, pieces):
    branches, rows, depth = own.shape
    chunk = pieces[0].shape[0]
    width = pieces[0].shape[1]

    def kernel(s_ref, own_ref, other_ref, *refs):
        w_refs, out_refs, held = refs[:5], refs[5:9], refs[9]
        image = s_ref[0]
        for slot in range(2):

            def part(h_ref):
                total = jnp.zeros((branches * rows, width), F32)
                for m, first, w_ref in ((0, 0, w_refs[0]), (1, 0, w_refs[1]), (2, 0, w_refs[2]), (3, 0, w_refs[3]), (3, 1, w_refs[4])):
                    size = w_ref.shape[0]
                    at = pl.multiple_of((image ^ m) * chunk + first * (chunk // 2), HD)
                    x = h_ref[:, :, pl.ds(at, size)].reshape(branches * rows, size)
                    total = total + jnp.dot(x, w_ref[...], preferred_element_type=F32)
                total = total.astype(BF)
                for hi in range(2):
                    held[hi * 2 + slot] = total[:, hi * HD : (hi + 1) * HD]

            @pl.when(s_ref[2 + slot] == 1)
            def _():
                part(own_ref)

            @pl.when(s_ref[2 + slot] != 1)
            def _():
                part(other_ref)

        for r, out in enumerate(out_refs):
            out[...] = held[(s_ref[1] + r) % 4]

    return call(
        kernel,
        [jax.ShapeDtypeStruct((branches * rows, HD), BF)] * 4,
        scalars,
        [own, other, *pieces],
        2 * 2 * branches * rows * depth * width,
        2 * (2 * branches * rows * depth + depth * width),
        [pltpu.VMEM((4, branches * rows, HD), BF)],
    )


def attend(scalars, guide, queries, caches, part):
    rows = queries[0].shape[0] // 2
    scale = 1.0 / math.sqrt(HD)
    count = len(queries)
    here = slice(part * HD, (part + 1) * HD)
    keys_all = sum(c.shape[0] * c.shape[3] for c in caches)

    def kernel(s_ref, g_ref, *refs):
        q_refs, c_refs, out, held = refs[:count], refs[count:-2], refs[-2], refs[-1]
        for r in range(count):

            @pl.when(s_ref[0] == r)
            def _():
                held[...] = q_refs[r][...]

        attended = []
        for b in range(2):
            q = held[b * rows : (b + 1) * rows]
            scores = []
            for c_ref in c_refs:
                for n in range(c_ref.shape[0]):
                    scores.append(
                        lax.dot_general(
                            q, c_ref[n, 0, b, :, here], (((1,), (1,)), ((), ())), preferred_element_type=F32
                        )
                        * scale
                    )
            top = jnp.max(scores[0], axis=-1, keepdims=True)
            for s in scores[1:]:
                top = jnp.maximum(top, jnp.max(s, axis=-1, keepdims=True))
            exps = [jnp.exp(s - top) for s in scores]
            total = jnp.sum(exps[0], axis=-1, keepdims=True)
            for e in exps[1:]:
                total = total + jnp.sum(e, axis=-1, keepdims=True)
            over = 1.0 / total
            result = jnp.zeros((rows, HD), F32)
            at = 0
            for c_ref in c_refs:
                for n in range(c_ref.shape[0]):
                    w = (exps[at] * over).astype(BF)
                    result = result + jnp.dot(w, c_ref[n, 1, b, :, here], preferred_element_type=F32)
                    at += 1
            attended.append(result)
        guided = attended[1] + g_ref[0] * (attended[0] - attended[1])
        out[...] = guided.astype(BF)

    def smem_kernel(s_ref, g_ref, *refs):
        kernel(s_ref, g_ref, *refs)

    return pl.pallas_call(
        smem_kernel,
        out_shape=jax.ShapeDtypeStruct((rows, HD), BF),
        in_specs=[SMEM_SPEC, SMEM_SPEC] + [VMEM_SPEC] * (count + len(caches)),
        out_specs=VMEM_SPEC,
        scratch_shapes=[pltpu.VMEM((2 * rows, HD), BF)],
        compiler_params=pltpu.CompilerParams(vmem_limit_bytes=VMEM_LIMIT),
        cost_estimate=pl.CostEstimate(
            flops=8 * rows * keys_all * HD,
            bytes_accessed=keys_all * 3 * HD * 8,
            transcendentals=2 * rows * keys_all,
        ),
    )(scalars, guide, *queries, *caches)


def paste(scalars, previous, mine, others, parts):
    rows, columns = previous.shape
    flat = [piece for part in mine for piece in part]
    rest = [piece for other in others for piece in other]

    def kernel(s_ref, prev_ref, *refs):
        out = refs[-1]
        out[...] = prev_ref[...]

        def put(k, m, piece):
            at = pl.multiple_of(((s_ref[0] ^ m) * parts + k) * HD, HD)
            out[:, pl.ds(at, HD)] = piece

        @pl.when(s_ref[1] == 1)
        def _():
            for k in range(parts):
                for m in range(GROUPS):
                    put(k, m, refs[k * GROUPS + m][...])

        for n in range(len(others)):

            @pl.when(s_ref[2 + n] == 1)
            def _():
                for k in range(parts):
                    for m in range(GROUPS):
                        put(k, m, refs[parts * GROUPS + n * parts + k][m])

    return call(
        kernel,
        jax.ShapeDtypeStruct((rows, columns), BF),
        scalars,
        [previous, *flat, *rest],
        0,
        2 * rows * columns * 4,
    )


def body(hidden, key_cache, value_cache, cached_out, w_query, guide, masked_tiles, mask_count):
    images = lax.axis_size("image")
    tokens = lax.axis_size("token")
    inner = key_cache.shape[3]
    heads = inner // HD
    parts = heads // GROUPS
    slots = masked_tiles.shape[1]
    layers = tokens // (2 * GROUPS)
    assert images == 4 and hidden.shape[1] == 1 and hidden.shape[2] == TILE
    assert tokens == layers * 2 * GROUPS and slots == 2 * layers and heads == parts * GROUPS

    image = lax.axis_index("image")
    token = lax.axis_index("token")
    core = token % 2
    chip = token // 2
    z = chip // layers
    layer = chip % layers
    tiles = masked_tiles[0]

    def over_image(x, m):
        return lax.ppermute(x, "image", [(i, i ^ m) for i in range(images)])

    def over_z(x, m):
        span = 2 * layers
        return lax.ppermute(x, "token", [(t, ((t // span) ^ m) * span + t % span) for t in range(tokens)])

    def over_core(x):
        return lax.ppermute(x, "token", [(t, t ^ 1) for t in range(tokens)])

    def to_targets(x, r):
        pairs = []
        for t in range(tokens):
            c, at, s = t % 2, (t // 2) % layers, t // 2 // layers
            goal = (s + r) % 4
            pairs.append((t, ((2 * c + goal // 2) * layers + at) * 2 + goal % 2))
        return lax.ppermute(x, "token", pairs)

    layer_groups = [
        [(s * layers + at) * 2 + c for at in range(layers)] for s in range(GROUPS) for c in range(2)
    ]
    group_groups = [list(range(s * layers * 2, (s + 1) * layers * 2)) for s in range(GROUPS)]

    packed = pack_weights(core[None], w_query, parts)
    half = w_query.shape[0] // 2
    weights = []
    for own in packed:
        by_x = over_image(own, 1)
        by_y = over_image(own, 2)
        far_first = over_image(by_x[:half], 2)
        far_last = over_image(by_y[half:], 1)
        weights.append([own, by_x, by_y, far_first, far_last])

    own_hidden = hidden[:, 0]
    other_hidden = over_core(own_hidden)

    blocks = pack_keys(z[None], key_cache[:, 0], value_cache[:, 0])
    arrived = [blocks[0]] + [over_z(blocks[m], m) for m in range(1, GROUPS)]
    gathered = jnp.concatenate(arrived, axis=2)
    if layers == 1:
        caches = [gathered[None], over_core(gathered)[None]]
    else:
        caches = [lax.all_gather(gathered, "token", axis_index_groups=group_groups)]

    my_slot = layer * 2 + core
    my_tile = tiles[my_slot]
    target = 2 * (z % 2) + core
    owner_z = my_tile // 2 // layers
    choice = (target - owner_z) % 4

    mine, others = [], []
    for k in range(parts):
        arrived_queries = None
        for at in range(layers):
            pair = tiles[2 * at : 2 * at + 2]
            is_own = (pair % 2 == core).astype(jnp.int32)
            scalars = jnp.concatenate([jnp.stack([image, z]).astype(jnp.int32), is_own])
            sent = project(scalars, own_hidden, other_hidden, weights[k])
            came = [to_targets(x, r) for r, x in enumerate(sent)]
            if layers > 1:
                holds = (tiles[2 * at + core] // 2) % layers == layer
                came = [
                    lax.psum(jnp.where(holds, x, jnp.zeros_like(x)), "token", axis_index_groups=layer_groups)
                    for x in came
                ]
            if arrived_queries is None:
                arrived_queries = came
            else:
                arrived_queries = [
                    jnp.where(layer == at, new, old) for new, old in zip(came, arrived_queries)
                ]
        guided = attend(choice[None], guide, arrived_queries, caches, k)
        pieces = [guided] + [over_z(guided, m) for m in range(1, GROUPS)]
        mine.append(pieces)
        stacked = jnp.stack(pieces)
        if layers == 1:
            others.append([over_core(stacked)])
        else:
            everyone = lax.all_gather(stacked, "token", axis_index_groups=group_groups)
            others.append([everyone[n] for n in range(slots)])

    in_use = jnp.arange(slots, dtype=jnp.int32) < mask_count[0]
    hit = ((tiles == token) & in_use).astype(jnp.int32)
    if layers == 1:
        flags = jnp.stack([z, hit[core], hit[1 - core]]).astype(jnp.int32)
    else:
        flags = jnp.concatenate([jnp.stack([z, hit[my_slot]]).astype(jnp.int32), hit])
    by_other = [[others[k][n] for k in range(parts)] for n in range(len(others[0]))]
    edited = paste(flags, cached_out[0], mine, by_other, parts)
    return edited[None]


def solution(mesh):
    return jax.shard_map(
        body,
        mesh=mesh,
        in_specs=(
            P(None, "image", "token", None),
            P(None, "image", "token", None),
            P(None, "image", "token", None),
            P("image", "token", None),
            P("image", None),
            P("image"),
            P("image", None),
            P("image"),
        ),
        out_specs=P("image", "token", None),
        check_vma=False,
    )
```

```python
import math

import jax
import jax.numpy as jnp
from jax import lax
from jax.experimental import pallas as pl
from jax.experimental.pallas import tpu as pltpu
from jax.sharding import PartitionSpec as P

HD = 128
TILE = 128
GROUPS = 4
BF = jnp.bfloat16
F32 = jnp.float32
MIB = 1024 * 1024

SMEM_SPEC = pl.BlockSpec(memory_space=pltpu.SMEM)
ANY_SPEC = pl.BlockSpec(memory_space=pl.ANY)


def call(kernel, out_shape, scalars, arrays, scratch=(), limit=4, aliases=None):
    many = isinstance(out_shape, (list, tuple))
    return pl.pallas_call(
        kernel,
        out_shape=out_shape,
        in_specs=[SMEM_SPEC] * len(scalars) + [ANY_SPEC] * len(arrays),
        out_specs=[ANY_SPEC] * len(out_shape) if many else ANY_SPEC,
        scratch_shapes=list(scratch),
        input_output_aliases=aliases or {},
        compiler_params=pltpu.CompilerParams(vmem_limit_bytes=limit * MIB),
        cost_estimate=pl.CostEstimate(flops=0, bytes_accessed=0, transcendentals=0),
    )(*scalars, *arrays)


def stays(x):
    return pltpu.with_memory_space_constraint(x, pltpu.HBM)


def run_all(copies):
    for copy in copies:
        copy.start()
    for copy in copies:
        copy.wait()


def after(x, *events):
    def kernel(*refs):
        pass

    return call(kernel, jax.ShapeDtypeStruct(x.shape, x.dtype), [], [x, *events], aliases={0: 0})


def pack_weights(core, w_query, heads, per_group, events=()):
    rows, columns = w_query.shape
    half = columns // 2
    width = len(heads) * HD
    assert heads == list(range(heads[0], heads[0] + len(heads)))

    def kernel(core_ref, w_ref, *refs):
        out, buf, sem, out_sem = refs[-4:]
        copies = []
        for hi in range(2):
            at = pl.multiple_of(core_ref[0] * half + (hi * per_group + heads[0]) * HD, HD)
            copies.append(
                pltpu.make_async_copy(
                    w_ref.at[:, pl.ds(at, width)], buf.at[:, hi * width : (hi + 1) * width], sem.at[hi]
                )
            )
        run_all(copies)
        run_all([pltpu.make_async_copy(buf, out, out_sem)])

    return call(
        kernel,
        jax.ShapeDtypeStruct((rows, 2 * width), BF),
        [core],
        [stays(w_query), *events],
        [pltpu.VMEM((rows, 2 * width), BF), pltpu.SemaphoreType.DMA((2,)), pltpu.SemaphoreType.DMA],
    )


def pack_caches(key_block, value_block, events=()):
    branches, tokens, columns = key_block.shape
    width = columns // GROUPS

    def kernel(k_ref, v_ref, *refs):
        out, buf, sem, out_sem = refs[-4:]
        copies = []
        for n, ref in enumerate((k_ref, v_ref)):
            for g in range(GROUPS):
                copies.append(
                    pltpu.make_async_copy(
                        ref.at[:, :, g * width : (g + 1) * width], buf.at[g, n], sem.at[n * GROUPS + g]
                    )
                )
        run_all(copies)
        run_all([pltpu.make_async_copy(buf, out, out_sem)])

    shape = (GROUPS, 2, branches, tokens, width)
    return call(
        kernel,
        jax.ShapeDtypeStruct(shape, BF),
        [],
        [stays(key_block), stays(value_block), *events],
        [pltpu.VMEM(shape, BF), pltpu.SemaphoreType.DMA((2 * GROUPS,)), pltpu.SemaphoreType.DMA],
    )


def halves(by_x, by_y, events=()):
    rows, width = by_x.shape
    half = rows // 2

    def kernel(x_ref, y_ref, *refs):
        first, last, buf, sem, out_sem = refs[-5:]
        sources = (x_ref.at[:half], y_ref.at[half:])
        run_all([pltpu.make_async_copy(ref, buf.at[n], sem.at[n]) for n, ref in enumerate(sources)])
        run_all([pltpu.make_async_copy(buf.at[n], ref, out_sem.at[n]) for n, ref in enumerate((first, last))])

    return call(
        kernel,
        [jax.ShapeDtypeStruct((half, width), BF)] * 2,
        [],
        [by_x, by_y, *events],
        [
            pltpu.VMEM((2, half, width), BF),
            pltpu.SemaphoreType.DMA((2,)),
            pltpu.SemaphoreType.DMA((2,)),
        ],
    )


def stack(pieces, events=()):
    shape = (sum(p.shape[0] for p in pieces), *pieces[0].shape[1:])

    def kernel(*refs):
        out, buf, sem, out_sem = refs[-4:]
        copies, at = [], 0
        for n, piece in enumerate(pieces):
            copies.append(pltpu.make_async_copy(refs[n], buf.at[at : at + piece.shape[0]], sem.at[n]))
            at += piece.shape[0]
        run_all(copies)
        run_all([pltpu.make_async_copy(buf, out, out_sem)])

    return call(
        kernel,
        jax.ShapeDtypeStruct(shape, BF),
        [],
        [*pieces, *events],
        [pltpu.VMEM(shape, BF), pltpu.SemaphoreType.DMA((len(pieces),)), pltpu.SemaphoreType.DMA],
    )


def project(scalars, own, other, pieces, places, before=None, events=()):
    branches, rows, depth = own.shape
    chunk = depth // 4
    width = pieces[0].shape[1]
    part = width // 2
    count = len(pieces)
    sizes = [p.shape[0] for p in pieces]
    last = before is not None
    outs = 4 if last else 1

    def kernel(s_ref, own_ref, other_ref, *refs):
        w_refs = refs[:count]
        h_buf, w_buf, t_buf, q_buf, sem, out_sem = refs[-6:]
        out_refs = refs[-6 - outs : -6]
        image = s_ref[0]
        columns = [
            pl.ds(pl.multiple_of((image ^ m) * chunk + row, HD), size) for (m, row), size in zip(places, sizes)
        ]
        firsts = [sum(sizes[:n]) for n in range(count)]
        loads = []
        for n in range(count):
            here = pl.ds(firsts[n], sizes[n])
            loads.append([pltpu.make_async_copy(w_refs[n], w_buf.at[here], sem.at[n, 2])])
            for slot in range(2):
                mine, theirs = [
                    pltpu.make_async_copy(ref.at[:, :, columns[n]], h_buf.at[slot, :, :, here], sem.at[n, slot])
                    for ref in (own_ref, other_ref)
                ]
                loads[n].append(mine)

                @pl.when(s_ref[2 + slot] == 1)
                def _():
                    mine.start()

                @pl.when(s_ref[2 + slot] != 1)
                def _():
                    theirs.start()

            loads[n][0].start()
        if last:
            sums = pltpu.make_async_copy(refs[count], t_buf, out_sem.at[0])
            sums.start()
        total = [jnp.zeros((branches * rows, width), F32) for _ in range(2)]
        for n in range(count):
            here = slice(firsts[n], firsts[n] + sizes[n])
            for load in loads[n]:
                load.wait()
            for slot in range(2):
                total[slot] = total[slot] + jnp.dot(
                    h_buf[slot, :, :, here].reshape(branches * rows, sizes[n]),
                    w_buf[here],
                    preferred_element_type=F32,
                )
        if last:
            sums.wait()
            for slot in range(2):
                done = (t_buf[slot] + total[slot]).astype(BF)
                for hi in range(2):
                    q_buf[hi * 2 + slot] = done[:, hi * part : (hi + 1) * part]
            run_all(
                [
                    pltpu.make_async_copy(q_buf.at[(s_ref[1] + r) % 4], out, out_sem.at[r])
                    for r, out in enumerate(out_refs)
                ]
            )
        else:
            for slot in range(2):
                t_buf[slot] = total[slot]
            run_all([pltpu.make_async_copy(t_buf, out_refs[0], out_sem.at[0])])

    sums = (2, branches * rows, width)
    return call(
        kernel,
        [jax.ShapeDtypeStruct((branches * rows, part), BF)] * 4 if last else jax.ShapeDtypeStruct(sums, F32),
        [scalars],
        [own, other, *pieces, *([before] if last else []), *events],
        [
            pltpu.VMEM((2, branches, rows, sum(sizes)), BF),
            pltpu.VMEM((sum(sizes), width), BF),
            pltpu.VMEM(sums, F32),
            pltpu.VMEM((4, branches * rows, part), BF),
            pltpu.SemaphoreType.DMA((count, 3)),
            pltpu.SemaphoreType.DMA((4,)),
        ],
        limit=16,
    )


def attend(scalars, guide, queries, caches, first_head, events=()):
    rows, width = queries[0].shape[0] // 2, queries[0].shape[1]
    scale = 1.0 / math.sqrt(HD)
    count, kept = len(queries), len(caches)
    here = slice(first_head * HD, first_head * HD + width)
    sizes = [c.shape[0] * c.shape[3] for c in caches]
    keys_all = sum(sizes)

    def kernel(s_ref, g_ref, *refs):
        q_refs, c_refs = refs[:count], refs[count : count + kept]
        out, q_buf, c_bufs, out_buf, sem = refs[-4 - kept], refs[-3 - kept], refs[-2 - kept : -2], refs[-2], refs[-1]
        for r in range(count):

            @pl.when(s_ref[0] == r)
            def _():
                pltpu.make_async_copy(q_refs[r], q_buf, sem.at[0]).start()

        loads = [
            pltpu.make_async_copy(c_ref.at[:, n, :, :, here], c_buf.at[n], sem.at[1 + 2 * i + n])
            for n in range(2)
            for i, (c_ref, c_buf) in enumerate(zip(c_refs, c_bufs))
        ]
        for load in loads:
            load.start()
        pltpu.make_async_copy(q_refs[0], q_buf, sem.at[0]).wait()
        for load in loads[:kept]:
            load.wait()
        for head in range(width // HD):
            at = slice(head * HD, (head + 1) * HD)
            attended = []
            for b in range(2):
                q = q_buf[b * rows : (b + 1) * rows, at]
                scores = [
                    lax.dot_general(
                        q,
                        c_buf[0, :, b, :, at].reshape(size, HD),
                        (((1,), (1,)), ((), ())),
                        preferred_element_type=F32,
                    )
                    * scale
                    for c_buf, size in zip(c_bufs, sizes)
                ]
                top = jnp.max(scores[0], axis=-1, keepdims=True)
                for s in scores[1:]:
                    top = jnp.maximum(top, jnp.max(s, axis=-1, keepdims=True))
                exps = [jnp.exp(s - top) for s in scores]
                total = jnp.sum(exps[0], axis=-1, keepdims=True)
                for e in exps[1:]:
                    total = total + jnp.sum(e, axis=-1, keepdims=True)
                over = 1.0 / total
                if head == 0 and b == 0:
                    for load in loads[kept:]:
                        load.wait()
                result = jnp.zeros((rows, HD), F32)
                for e, c_buf, size in zip(exps, c_bufs, sizes):
                    w = (e * over).astype(BF)
                    result = result + jnp.dot(
                        w, c_buf[1, :, b, :, at].reshape(size, HD), preferred_element_type=F32
                    )
                attended.append(result)
            guided = attended[1] + g_ref[0] * (attended[0] - attended[1])
            out_buf[:, at] = guided.astype(BF)
        run_all([pltpu.make_async_copy(out_buf, out, sem.at[0])])

    return call(
        kernel,
        jax.ShapeDtypeStruct((rows, width), BF),
        [scalars, guide],
        [*queries, *caches, *events],
        [pltpu.VMEM((2 * rows, width), BF)]
        + [pltpu.VMEM((2, c.shape[0], c.shape[2], c.shape[3], width), BF) for c in caches]
        + [pltpu.VMEM((rows, width), BF), pltpu.SemaphoreType.DMA((1 + 2 * kept,))],
        limit=16 + 8 * (keys_all // 1024),
    )


def paste(scalars, previous, mine, others, firsts, per_group):
    rows, columns = previous.shape
    flat = [piece for part in mine for piece in part]
    rest = [piece for other in others for piece in other]
    parts = len(firsts)

    def kernel(s_ref, prev_ref, *refs):
        out, buf, sem, out_sem = refs[-4:]

        def place(k, m, width):
            at = pl.multiple_of(((s_ref[0] ^ m) * per_group + firsts[k]) * HD, HD)
            return buf.at[:, pl.ds(at, width)]

        taken = s_ref[1]
        for n in range(len(others)):
            taken = taken + s_ref[2 + n]

        @pl.when(taken == 0)
        def _():
            run_all([pltpu.make_async_copy(prev_ref, buf, sem.at[0])])

        @pl.when(s_ref[1] == 1)
        def _():
            copies = []
            for k in range(parts):
                for m in range(GROUPS):
                    piece = refs[k * GROUPS + m]
                    copies.append(
                        pltpu.make_async_copy(piece, place(k, m, piece.shape[1]), sem.at[k * GROUPS + m])
                    )
            run_all(copies)

        for n in range(len(others)):

            @pl.when(s_ref[2 + n] == 1)
            def _():
                copies = []
                for k in range(parts):
                    piece = refs[parts * GROUPS + n * parts + k]
                    for m in range(GROUPS):
                        copies.append(
                            pltpu.make_async_copy(
                                piece.at[m], place(k, m, piece.shape[2]), sem.at[k * GROUPS + m]
                            )
                        )
                run_all(copies)

        run_all([pltpu.make_async_copy(buf, out, out_sem)])

    return call(
        kernel,
        jax.ShapeDtypeStruct((rows, columns), BF),
        [scalars],
        [stays(previous), *flat, *rest],
        [
            pltpu.VMEM((rows, columns), BF),
            pltpu.SemaphoreType.DMA((parts * GROUPS,)),
            pltpu.SemaphoreType.DMA,
        ],
    )


def body(hidden, key_cache, value_cache, cached_out, w_query, guide, masked_tiles, mask_count):
    images = lax.axis_size("image")
    tokens = lax.axis_size("token")
    heads = key_cache.shape[3] // HD
    per_group = heads // GROUPS
    slots = masked_tiles.shape[1]
    layers = tokens // (2 * GROUPS)
    assert images == 4 and hidden.shape[1] == 1 and hidden.shape[2] == TILE
    assert tokens == layers * 2 * GROUPS and slots == 2 * layers and heads == per_group * GROUPS

    image = lax.axis_index("image")
    token = lax.axis_index("token")
    core = token % 2
    chip = token // 2
    z = chip // layers
    layer = chip % layers
    tiles = masked_tiles[0]

    def over_image(x, m):
        return lax.ppermute(x, "image", [(i, i ^ m) for i in range(images)])

    def over_z(x, m):
        span = 2 * layers
        return lax.ppermute(x, "token", [(t, ((t // span) ^ m) * span + t % span) for t in range(tokens)])

    def over_core(x):
        return lax.ppermute(x, "token", [(t, t ^ 1) for t in range(tokens)])

    def to_targets(x, r):
        pairs = []
        for t in range(tokens):
            c, at, s = t % 2, (t // 2) % layers, t // 2 // layers
            goal = (s + r) % 4
            pairs.append((t, ((2 * c + goal // 2) * layers + at) * 2 + goal % 2))
        return lax.ppermute(x, "token", pairs)

    layer_groups = [
        [(s * layers + at) * 2 + c for at in range(layers)] for s in range(GROUPS) for c in range(2)
    ]
    group_groups = [list(range(s * layers * 2, (s + 1) * layers * 2)) for s in range(GROUPS)]
    z_groups = [[s * 2 * layers + at for s in range(GROUPS)] for at in range(2 * layers)]

    plan = [list(range(per_group))]
    parts = len(plan)
    firsts = [p[0] for p in plan]
    half = w_query.shape[0] // 2
    near_places = [(0, 0), (1, 0), (2, 0)]
    far_places = [(3, 0), (3, half)]

    own_hidden = hidden[:, 0]
    other_hidden = over_core(own_hidden)

    def near(k, *events):
        own = pack_weights(core[None], w_query, plan[k], per_group, events)
        return [own, over_image(own, 1), over_image(own, 2)]

    def far(k, *events):
        first, last = halves(weights[k][1], weights[k][2], events)
        return [over_image(first, 2), over_image(last, 1)], first

    my_slot = layer * 2 + core
    my_tile = tiles[my_slot]
    target = 2 * (z % 2) + core
    owner_z = my_tile // 2 // layers
    choice = (target - owner_z) % 4

    def scalars_of(at):
        pair = tiles[2 * at : 2 * at + 2]
        return jnp.concatenate([jnp.stack([image, z]).astype(jnp.int32), (pair % 2 == core).astype(jnp.int32)])

    def begin(k, *events):
        return [
            project(scalars_of(at), own_hidden, other_hidden, weights[k], near_places, events=events)
            for at in range(layers)
        ]

    def finish(k, sums, came_far, *events):
        result = None
        for at in range(layers):
            sent = project(
                scalars_of(at), own_hidden, other_hidden, came_far, far_places, sums[at], events=events
            )
            came = [to_targets(x, r) for r, x in enumerate(sent)]
            if layers > 1:
                holds = (tiles[2 * at + core] // 2) % layers == layer
                came = [
                    lax.psum(jnp.where(holds, x, jnp.zeros_like(x)), "token", axis_index_groups=layer_groups)
                    for x in came
                ]
            if result is None:
                result = came
            else:
                result = [jnp.where(layer == at, new, old) for new, old in zip(came, result)]
        return result, sent[0]

    weights = [near(0)]

    blocks = pack_caches(key_cache[:, 0], value_cache[:, 0], weights[0][:1])
    gathered = lax.all_to_all(blocks, "token", 0, 0, axis_index_groups=z_groups)

    far_0, event = far(0, blocks)
    sums_0 = begin(0, event)
    queries_0, event = finish(0, sums_0, far_0)
    queries = [queries_0]

    gathered = after(gathered, event)
    if layers == 1:
        caches = [gathered, over_core(gathered)]
    else:
        everyone = lax.all_gather(gathered, "token", axis_index_groups=group_groups)
        caches = [everyone.reshape(-1, *gathered.shape[1:])]

    mine, others = [], []
    for k in range(parts):
        guided = attend(choice[None], guide, queries[k], caches, firsts[k])
        pieces = [guided] + [over_z(guided, m) for m in range(1, GROUPS)]
        mine.append(pieces)
        stacked = stack([p[None] for p in pieces])
        if layers == 1:
            others.append([over_core(stacked)])
        else:
            everyone = lax.all_gather(stacked, "token", axis_index_groups=group_groups)
            others.append([everyone[n] for n in range(slots)])

    in_use = jnp.arange(slots, dtype=jnp.int32) < mask_count[0]
    hit = ((tiles == token) & in_use).astype(jnp.int32)
    own_hit = hit[my_slot]
    other_hits = hit[1 - core][None] if layers == 1 else jnp.where(jnp.arange(slots) == my_slot, 0, hit)
    flags = jnp.concatenate([jnp.stack([z, own_hit]).astype(jnp.int32), other_hits])
    by_other = [[others[k][n] for k in range(parts)] for n in range(len(others[0]))]
    edited = paste(flags, cached_out[0], mine, by_other, firsts, per_group)
    return edited[None]


def solution(mesh):
    return jax.shard_map(
        body,
        mesh=mesh,
        in_specs=(
            P(None, "image", "token", None),
            P(None, "image", "token", None),
            P(None, "image", "token", None),
            P("image", "token", None),
            P("image", None),
            P("image"),
            P("image", None),
            P("image"),
        ),
        out_specs=P("image", "token", None),
        check_vma=False,
    )
```

```python
import math

import jax
import jax.numpy as jnp
from jax import lax
from jax.experimental import pallas as pl
from jax.experimental.pallas import tpu as pltpu
from jax.sharding import PartitionSpec as P

HD = 128
TILE = 128
GROUPS = 4
BF = jnp.bfloat16
F32 = jnp.float32
MIB = 1024 * 1024

SMEM_SPEC = pl.BlockSpec(memory_space=pltpu.SMEM)
ANY_SPEC = pl.BlockSpec(memory_space=pl.ANY)
VMEM_SPEC = pl.BlockSpec(memory_space=pltpu.VMEM)


def call(kernel, out_shape, scalars, arrays, scratch=(), limit=4, aliases=None, spec=ANY_SPEC, out_spec=ANY_SPEC, flops=0):
    many = isinstance(out_shape, (list, tuple))
    return pl.pallas_call(
        kernel,
        out_shape=out_shape,
        in_specs=[SMEM_SPEC] * len(scalars) + (spec if isinstance(spec, list) else [spec] * len(arrays)),
        out_specs=[out_spec] * len(out_shape) if many else out_spec,
        scratch_shapes=list(scratch),
        input_output_aliases=aliases or {},
        compiler_params=pltpu.CompilerParams(vmem_limit_bytes=limit * MIB),
        cost_estimate=pl.CostEstimate(flops=flops, bytes_accessed=0, transcendentals=0),
    )(*scalars, *arrays)


def stays(x):
    return pltpu.with_memory_space_constraint(x, pltpu.HBM)


def run_all(copies):
    for copy in copies:
        copy.start()
    for copy in copies:
        copy.wait()


def run_both(loads, stores):
    for load in loads:
        load.start()
    for load, store in zip(loads, stores):
        load.wait()
        store.start()
    for store in stores:
        store.wait()


def after(x, *events):
    def kernel(*refs):
        pass

    return call(kernel, jax.ShapeDtypeStruct(x.shape, x.dtype), [], [x, *events], aliases={0: 0})


def pack_weights(core, w_query, heads_of, events=()):
    rows, columns = w_query.shape
    count = len(heads_of(0))
    shape = (rows, count * HD)

    def kernel(core_ref, w_ref, *refs):
        out, buf, sem, out_sem = refs[-4:]
        loads, stores = [], []
        for n, head in enumerate(heads_of(core_ref[0])):
            here = slice(n * HD, (n + 1) * HD)
            at = pl.ds(pl.multiple_of(head * HD, HD), HD)
            loads.append(pltpu.make_async_copy(w_ref.at[:, at], buf.at[:, here], sem.at[n]))
            stores.append(pltpu.make_async_copy(buf.at[:, here], out.at[:, here], out_sem.at[n]))
        run_both(loads, stores)

    return call(
        kernel,
        jax.ShapeDtypeStruct(shape, BF),
        [core],
        [stays(w_query), *events],
        [pltpu.VMEM(shape, BF), pltpu.SemaphoreType.DMA((count,)), pltpu.SemaphoreType.DMA((count,))],
    )


def pack_caches(key_block, value_block, events=()):
    branches, tokens, columns = key_block.shape
    width = columns // GROUPS

    def kernel(k_ref, v_ref, *refs):
        out, buf, sem, out_sem = refs[-4:]
        loads, stores = [], []
        for n, ref in enumerate((k_ref, v_ref)):
            for g in range(GROUPS):
                here = buf.at[g, n]
                loads.append(
                    pltpu.make_async_copy(
                        ref.at[:, :, g * width : (g + 1) * width], here, sem.at[n * GROUPS + g]
                    )
                )
                stores.append(pltpu.make_async_copy(here, out.at[g, n], out_sem.at[n * GROUPS + g]))
        run_both(loads, stores)

    shape = (GROUPS, 2, branches, tokens, width)
    return call(
        kernel,
        jax.ShapeDtypeStruct(shape, BF),
        [],
        [stays(key_block), stays(value_block), *events],
        [pltpu.VMEM(shape, BF), pltpu.SemaphoreType.DMA((2 * GROUPS,)), pltpu.SemaphoreType.DMA((2 * GROUPS,))],
    )


def halves(flags, by_x, by_y, events=()):
    rows, width = by_x.shape
    half = rows // 2

    def kernel(_, x_ref, y_ref, *refs):
        first, last, buf, sem, out_sem = refs[-5:]
        sources = (x_ref.at[:half], y_ref.at[half:])
        run_all([pltpu.make_async_copy(ref, buf.at[n], sem.at[n]) for n, ref in enumerate(sources)])
        run_all([pltpu.make_async_copy(buf.at[n], ref, out_sem.at[n]) for n, ref in enumerate((first, last))])

    return call(
        kernel,
        [jax.ShapeDtypeStruct((half, width), BF)] * 2,
        [flags],
        [by_x, by_y, *events],
        [
            pltpu.VMEM((2, half, width), BF),
            pltpu.SemaphoreType.DMA((2,)),
            pltpu.SemaphoreType.DMA((2,)),
        ],
    )


def stack(pieces):
    def kernel(*refs):
        for n in range(len(pieces)):
            refs[-1][n] = refs[n][...]

    return call(
        kernel,
        jax.ShapeDtypeStruct((len(pieces), *pieces[0].shape), BF),
        [],
        pieces,
        spec=VMEM_SPEC,
        out_spec=VMEM_SPEC,
    )


def begin_project(flags, at, own, other, pieces, far_rows, events=()):
    branches, rows, depth = own.shape
    chunk, width = pieces[0].shape
    count = len(pieces)
    both = branches * rows

    def kernel(s_ref, own_ref, other_ref, *refs):
        w_refs = refs[:count]
        t_ref, far_ref, h_buf, w_buf, sem = refs[-5:]
        loads = []
        for n in range(count + 1):
            columns = pl.ds(pl.multiple_of((s_ref[0] ^ n) * chunk, HD), chunk)
            loads.append([])
            if n < count:
                loads[n].append(pltpu.make_async_copy(w_refs[n], w_buf.at[n], sem.at[n, 2]))
                loads[n][0].start()
            for slot in range(2):
                for b in range(branches):
                    there = h_buf.at[n, slot] if n < count else far_ref.at[slot]
                    there = there.at[b * rows : (b + 1) * rows]
                    mine, theirs = [
                        pltpu.make_async_copy(ref.at[b, :, columns], there, sem.at[n, slot])
                        for ref in (own_ref, other_ref)
                    ]
                    loads[n].append(mine)

                    @pl.when(s_ref[at + slot] == 1)
                    def _():
                        mine.start()

                    @pl.when(s_ref[at + slot] != 1)
                    def _():
                        theirs.start()

        for n in range(count):
            for load in loads[n]:
                load.wait()
            for slot in range(2):
                product = jnp.dot(h_buf[n, slot], w_buf[n], preferred_element_type=F32)
                if n == 0:
                    t_ref[slot] = product
                else:
                    t_ref[slot] += product
        for load in loads[count]:
            load.wait()

    return call(
        kernel,
        [jax.ShapeDtypeStruct((2, both, width), F32), jax.ShapeDtypeStruct((2, both, far_rows), BF)],
        [flags],
        [own, other, *pieces, *events],
        [
            pltpu.VMEM((count, 2, both, chunk), BF),
            pltpu.VMEM((count, chunk, width), BF),
            pltpu.SemaphoreType.DMA((count + 1, 3)),
        ],
        limit=16,
        out_spec=VMEM_SPEC,
        flops=25_000_000_000,
    )


def finish_project(flags, sums, rows_far, pieces, earlier=None, events=()):
    _, both, width = sums.shape
    part = width // 2
    count = len(pieces)
    last = earlier is not None
    before = earlier.shape[2] if last else 0

    def kernel(s_ref, t_ref, far_ref, *refs):
        w_refs = refs[:count]
        q_buf = refs[-1]
        for slot in range(2):
            total, first = t_ref[slot], 0
            for w_ref in w_refs:
                size = w_ref.shape[0]
                total = total + jnp.dot(
                    far_ref[slot, :, first : first + size], w_ref[...], preferred_element_type=F32
                )
                first += size
            total = total.astype(BF)
            for hi in range(2):
                q_buf[hi * 2 + slot] = total[:, hi * part : (hi + 1) * part]
        if last:
            for r, out in enumerate(refs[-5:-1]):
                target = (s_ref[1] + r) % 4
                out[:, :before] = refs[count][target]
                out[:, before:] = q_buf[target]

    whole = jax.ShapeDtypeStruct((4, both, part), BF)
    piece = jax.ShapeDtypeStruct((both, before + part), BF)
    return call(
        kernel,
        [piece] * 4 if last else whole,
        [flags],
        [sums, rows_far, *pieces, *([earlier] if last else []), *events],
        [pltpu.VMEM((4, both, part), BF)] if last else [],
        limit=8,
        spec=[VMEM_SPEC] * (2 + count + last) + [ANY_SPEC] * len(events),
        out_spec=VMEM_SPEC,
    )


def attend(flags, guide, queries, caches):
    count, parts, kept = len(queries[0]), len(queries), len(caches)
    rows = queries[0][0].shape[0] // 2
    widths = [part[0].shape[1] for part in queries]
    scale = 1.0 / math.sqrt(HD)
    sizes = [c.shape[0] * c.shape[3] for c in caches]
    keys_all = sum(sizes)

    def kernel(s_ref, g_ref, *refs):
        q_refs, c_refs = refs[: parts * count], refs[parts * count : parts * count + kept]
        out, q_buf = refs[-2:]
        for r in range(count):

            @pl.when(s_ref[2] == r)
            def _():
                first = 0
                for k in range(parts):
                    q_buf[:, first : first + widths[k]] = q_refs[k * count + r][...]
                    first += widths[k]

        for head in range(sum(widths) // HD):
            at = slice(head * HD, (head + 1) * HD)
            attended = []
            for b in range(2):
                q = q_buf[b * rows : (b + 1) * rows, at]
                scores = [
                    lax.dot_general(
                        q,
                        c_ref[:, 0, b, :, at].reshape(size, HD),
                        (((1,), (1,)), ((), ())),
                        preferred_element_type=F32,
                    )
                    * scale
                    for c_ref, size in zip(c_refs, sizes)
                ]
                top = jnp.max(scores[0], axis=-1, keepdims=True)
                for s in scores[1:]:
                    top = jnp.maximum(top, jnp.max(s, axis=-1, keepdims=True))
                exps = [jnp.exp(s - top) for s in scores]
                total = jnp.sum(exps[0], axis=-1, keepdims=True)
                for e in exps[1:]:
                    total = total + jnp.sum(e, axis=-1, keepdims=True)
                over = 1.0 / total
                result = jnp.zeros((rows, HD), F32)
                for e, c_ref, size in zip(exps, c_refs, sizes):
                    w = (e * over).astype(BF)
                    result = result + jnp.dot(
                        w, c_ref[:, 1, b, :, at].reshape(size, HD), preferred_element_type=F32
                    )
                attended.append(result)
            guided = attended[1] + g_ref[0] * (attended[0] - attended[1])
            out[:, at] = guided.astype(BF)

    return call(
        kernel,
        jax.ShapeDtypeStruct((rows, sum(widths)), BF),
        [flags, guide],
        [q for part in queries for q in part] + caches,
        [pltpu.VMEM((2 * rows, sum(widths)), BF)],
        limit=8 + 8 * (keys_all // 1024),
        spec=VMEM_SPEC,
        out_spec=VMEM_SPEC,
    )


def paste(flags, previous, mine, others):
    rows, columns = previous.shape
    width = columns // GROUPS

    def kernel(s_ref, prev_ref, *refs):
        out, sem = refs[-2:]

        def place(m):
            return out.at[:, pl.ds(pl.multiple_of((s_ref[1] ^ m) * width, HD), width)]

        taken = s_ref[3]
        for n in range(len(others)):
            taken = taken + s_ref[4 + n]

        @pl.when(taken == 0)
        def _():
            run_all([pltpu.make_async_copy(prev_ref, out, sem.at[0])])

        @pl.when(s_ref[3] == 1)
        def _():
            run_all([pltpu.make_async_copy(refs[m], place(m), sem.at[m]) for m in range(GROUPS)])

        for n in range(len(others)):

            @pl.when(s_ref[4 + n] == 1)
            def _():
                run_all(
                    [pltpu.make_async_copy(refs[GROUPS + n].at[m], place(m), sem.at[m]) for m in range(GROUPS)]
                )

    return call(
        kernel,
        jax.ShapeDtypeStruct((rows, columns), BF),
        [flags],
        [previous, *mine, *others],
        [pltpu.SemaphoreType.DMA((GROUPS,))],
        spec=VMEM_SPEC,
    )


def body(hidden, key_cache, value_cache, cached_out, w_query, guide, masked_tiles, mask_count):
    images = lax.axis_size("image")
    tokens = lax.axis_size("token")
    heads = key_cache.shape[3] // HD
    per_group = heads // GROUPS
    slots = masked_tiles.shape[1]
    layers = tokens // (2 * GROUPS)
    assert images == 4 and hidden.shape[1] == 1 and hidden.shape[2] == TILE
    assert tokens == layers * 2 * GROUPS and slots == 2 * layers and heads == per_group * GROUPS

    image = lax.axis_index("image")
    token = lax.axis_index("token")
    core = token % 2
    chip = token // 2
    z = chip // layers
    layer = chip % layers
    tiles = masked_tiles[0]

    def over_image(x, m):
        return lax.ppermute(x, "image", [(i, i ^ m) for i in range(images)])

    def over_z(x, m):
        span = 2 * layers
        return lax.ppermute(x, "token", [(t, ((t // span) ^ m) * span + t % span) for t in range(tokens)])

    def over_core(x):
        return lax.ppermute(x, "token", [(t, t ^ 1) for t in range(tokens)])

    def to_targets(x, r):
        pairs = []
        for t in range(tokens):
            c, at, s = t % 2, (t // 2) % layers, t // 2 // layers
            goal = (s + r) % 4
            pairs.append((t, ((2 * c + goal // 2) * layers + at) * 2 + goal % 2))
        return lax.ppermute(x, "token", pairs)

    layer_groups = [
        [(s * layers + at) * 2 + c for at in range(layers)] for s in range(GROUPS) for c in range(2)
    ]
    group_groups = [list(range(s * layers * 2, (s + 1) * layers * 2)) for s in range(GROUPS)]
    z_groups = [[s * 2 * layers + at for s in range(GROUPS)] for at in range(2 * layers)]

    plan = [list(range(per_group - 1)), [per_group - 1]]

    def part_heads(k):
        return lambda c: [(2 * c + hi) * per_group + head for hi in range(2) for head in plan[k]]

    half = w_query.shape[0] // 2
    own_hidden = hidden[:, 0]
    other_hidden = over_core(own_hidden)

    my_slot = layer * 2 + core
    my_tile = tiles[my_slot]
    target = 2 * (z % 2) + core
    choice = (target - my_tile // 2 // layers) % 4
    in_use = jnp.arange(slots, dtype=jnp.int32) < mask_count[0]
    hit = ((tiles == token) & in_use).astype(jnp.int32)
    other_hits = hit[1 - core][None] if layers == 1 else jnp.where(jnp.arange(slots) == my_slot, 0, hit)
    is_own = (tiles % 2 == core).astype(jnp.int32)
    flags = jnp.concatenate(
        [jnp.stack([image, z, choice, hit[my_slot]]).astype(jnp.int32), other_hits, is_own]
    )
    pairs_from = 4 + other_hits.shape[0]

    def near(k, *events):
        own = pack_weights(core[None], w_query, part_heads(k), events)
        return [own, over_image(own, 1), over_image(own, 2)]

    def far(k, *events):
        first, last = halves(flags, weights[k][1], weights[k][2], events)
        return [over_image(first, 2), over_image(last, 1)], first

    def begin(k, *events):
        return [
            begin_project(
                flags, pairs_from + 2 * at, own_hidden, other_hidden, weights[k], w_query.shape[0], events
            )
            for at in range(layers)
        ]

    def finish(begun_0, far_0, begun_1, far_1, *events):
        result = None
        for at in range(layers):
            first = finish_project(flags, *begun_0[at], far_0, events=events)
            sent = finish_project(flags, *begun_1[at], far_1, first)
            came = [to_targets(x, r) for r, x in enumerate(sent)]
            if layers > 1:
                holds = (tiles[2 * at + core] // 2) % layers == layer
                came = [
                    lax.psum(jnp.where(holds, x, jnp.zeros_like(x)), "token", axis_index_groups=layer_groups)
                    for x in came
                ]
            if result is None:
                result = came
            else:
                result = [jnp.where(layer == at, new, old) for new, old in zip(came, result)]
        return result, sent[0]

    weights = [near(0)]
    blocks = pack_caches(key_cache[:, 0], value_cache[:, 0], weights[0][:1])
    gathered = lax.all_to_all(blocks, "token", 0, 0, axis_index_groups=z_groups)
    weights.append(near(1, blocks))
    far_0, event = far(0, weights[1][0])
    begun_0 = begin(0, event)
    far_1, event = far(1, begun_0[0][1])
    begun_1 = begin(1, event)
    queries, event = finish(begun_0, far_0, begun_1, far_1, begun_1[0][1])

    gathered = after(gathered, event, queries[0], queries[1])
    if layers == 1:
        caches = [gathered, over_core(gathered)]
    else:
        everyone = lax.all_gather(gathered, "token", axis_index_groups=group_groups)
        caches = [everyone.reshape(-1, *gathered.shape[1:])]

    guided = attend(flags, guide, [queries], caches)
    mine = [guided] + [over_z(guided, m) for m in range(1, GROUPS)]
    stacked = stack(mine)
    if layers == 1:
        others = [over_core(stacked)]
    else:
        everyone = lax.all_gather(stacked, "token", axis_index_groups=group_groups)
        others = [everyone[n] for n in range(slots)]
    return paste(flags, cached_out[0], mine, others)[None]


def solution(mesh):
    return jax.shard_map(
        body,
        mesh=mesh,
        in_specs=(
            P(None, "image", "token", None),
            P(None, "image", "token", None),
            P(None, "image", "token", None),
            P("image", "token", None),
            P("image", None),
            P("image"),
            P("image", None),
            P("image"),
        ),
        out_specs=P("image", "token", None),
        check_vma=False,
    )
```

```python
import math

import jax
import jax.numpy as jnp
from jax import lax
from jax.experimental import pallas as pl
from jax.experimental.pallas import tpu as pltpu
from jax.sharding import PartitionSpec as P

HD = 128
TILE = 128
GROUPS = 4
BF = jnp.bfloat16
F32 = jnp.float32
MIB = 1024 * 1024

SMEM_SPEC = pl.BlockSpec(memory_space=pltpu.SMEM)
ANY_SPEC = pl.BlockSpec(memory_space=pl.ANY)
VMEM_SPEC = pl.BlockSpec(memory_space=pltpu.VMEM)


def call(kernel, out_shape, scalars, arrays, scratch=(), limit=4, aliases=None, spec=ANY_SPEC, out_spec=ANY_SPEC, flops=0):
    many = isinstance(out_shape, (list, tuple))
    return pl.pallas_call(
        kernel,
        out_shape=out_shape,
        in_specs=[SMEM_SPEC] * len(scalars) + (spec if isinstance(spec, list) else [spec] * len(arrays)),
        out_specs=[out_spec] * len(out_shape) if many else out_spec,
        scratch_shapes=list(scratch),
        input_output_aliases=aliases or {},
        compiler_params=pltpu.CompilerParams(vmem_limit_bytes=limit * MIB),
        cost_estimate=pl.CostEstimate(flops=flops, bytes_accessed=0, transcendentals=0),
    )(*scalars, *arrays)


def stays(x):
    return pltpu.with_memory_space_constraint(x, pltpu.HBM)


def run_all(copies):
    for copy in copies:
        copy.start()
    for copy in copies:
        copy.wait()


def run_both(loads, stores):
    for load in loads:
        load.start()
    for load, store in zip(loads, stores):
        load.wait()
        store.start()
    for store in stores:
        store.wait()


def after(x, *events):
    def kernel(*refs):
        pass

    return call(kernel, jax.ShapeDtypeStruct(x.shape, x.dtype), [], [x, *events], aliases={0: 0})


def pack_weights(core, w_query, heads_of, events=()):
    rows, columns = w_query.shape
    count = len(heads_of(0))
    shape = (rows, count * HD)

    def kernel(core_ref, w_ref, *refs):
        out, buf, sem, out_sem = refs[-4:]
        loads, stores = [], []
        for n, head in enumerate(heads_of(core_ref[0])):
            here = slice(n * HD, (n + 1) * HD)
            at = pl.ds(pl.multiple_of(head * HD, HD), HD)
            loads.append(pltpu.make_async_copy(w_ref.at[:, at], buf.at[:, here], sem.at[n]))
            stores.append(pltpu.make_async_copy(buf.at[:, here], out.at[:, here], out_sem.at[n]))
        run_both(loads, stores)

    return call(
        kernel,
        jax.ShapeDtypeStruct(shape, BF),
        [core],
        [stays(w_query), *events],
        [pltpu.VMEM(shape, BF), pltpu.SemaphoreType.DMA((count,)), pltpu.SemaphoreType.DMA((count,))],
    )


def pack_caches(key_block, value_block, events=()):
    branches, tokens, columns = key_block.shape
    width = columns // GROUPS

    def kernel(k_ref, v_ref, *refs):
        out, buf, sem, out_sem = refs[-4:]
        loads, stores = [], []
        for n, ref in enumerate((k_ref, v_ref)):
            for g in range(GROUPS):
                here = buf.at[g, n]
                loads.append(
                    pltpu.make_async_copy(
                        ref.at[:, :, g * width : (g + 1) * width], here, sem.at[n * GROUPS + g]
                    )
                )
                stores.append(pltpu.make_async_copy(here, out.at[g, n], out_sem.at[n * GROUPS + g]))
        run_both(loads, stores)

    shape = (GROUPS, 2, branches, tokens, width)
    return call(
        kernel,
        jax.ShapeDtypeStruct(shape, BF),
        [],
        [stays(key_block), stays(value_block), *events],
        [pltpu.VMEM(shape, BF), pltpu.SemaphoreType.DMA((2 * GROUPS,)), pltpu.SemaphoreType.DMA((2 * GROUPS,))],
    )


def halves(flags, by_x, by_y, events=()):
    rows, width = by_x.shape
    half = rows // 2

    def kernel(_, x_ref, y_ref, *refs):
        first, last, buf, sem, out_sem = refs[-5:]
        sources = (x_ref.at[:half], y_ref.at[half:])
        run_all([pltpu.make_async_copy(ref, buf.at[n], sem.at[n]) for n, ref in enumerate(sources)])
        run_all([pltpu.make_async_copy(buf.at[n], ref, out_sem.at[n]) for n, ref in enumerate((first, last))])

    return call(
        kernel,
        [jax.ShapeDtypeStruct((half, width), BF)] * 2,
        [flags],
        [by_x, by_y, *events],
        [
            pltpu.VMEM((2, half, width), BF),
            pltpu.SemaphoreType.DMA((2,)),
            pltpu.SemaphoreType.DMA((2,)),
        ],
    )


def begin_project(flags, at, own, other, pieces, far_rows, events=()):
    branches, rows, depth = own.shape
    chunk, width = pieces[0].shape
    count = len(pieces)
    both = branches * rows

    def kernel(s_ref, own_ref, other_ref, *refs):
        w_refs = refs[:count]
        t_ref, far_ref, h_buf, w_buf, sem = refs[-5:]
        loads = []
        for n in range(count + 1):
            columns = pl.ds(pl.multiple_of((s_ref[0] ^ n) * chunk, HD), chunk)
            loads.append([])
            if n < count:
                loads[n].append(pltpu.make_async_copy(w_refs[n], w_buf.at[n], sem.at[n, 2]))
                loads[n][0].start()
            for slot in range(2):
                for b in range(branches):
                    there = h_buf.at[n, slot] if n < count else far_ref.at[slot]
                    there = there.at[b * rows : (b + 1) * rows]
                    mine, theirs = [
                        pltpu.make_async_copy(ref.at[b, :, columns], there, sem.at[n, slot])
                        for ref in (own_ref, other_ref)
                    ]
                    loads[n].append(mine)

                    @pl.when(s_ref[at + slot] == 1)
                    def _():
                        mine.start()

                    @pl.when(s_ref[at + slot] != 1)
                    def _():
                        theirs.start()

        for n in range(count):
            for load in loads[n]:
                load.wait()
            for slot in range(2):
                product = jnp.dot(h_buf[n, slot], w_buf[n], preferred_element_type=F32)
                if n == 0:
                    t_ref[slot] = product
                else:
                    t_ref[slot] += product
        for load in loads[count]:
            load.wait()

    return call(
        kernel,
        [jax.ShapeDtypeStruct((2, both, width), F32), jax.ShapeDtypeStruct((2, both, far_rows), BF)],
        [flags],
        [own, other, *pieces, *events],
        [
            pltpu.VMEM((count, 2, both, chunk), BF),
            pltpu.VMEM((count, chunk, width), BF),
            pltpu.SemaphoreType.DMA((count + 1, 3)),
        ],
        limit=16,
        out_spec=VMEM_SPEC,
        flops=25_000_000_000,
    )


def finish_project(flags, first_at, sums, rows_far, pieces, earlier=(), events=()):
    _, both, width = sums.shape
    part = width // 2
    count, kept = len(pieces), len(earlier)
    before = earlier[0].shape[1] if earlier else 0

    def kernel(s_ref, t_ref, far_ref, *refs):
        w_refs, e_refs, out_refs = refs[:count], refs[count : count + kept], refs[-4:]
        for n in range(2):
            slot = s_ref[first_at] if n == 0 else 1
            total, first = t_ref[slot], 0
            for w_ref in w_refs:
                size = w_ref.shape[0]
                total = total + jnp.dot(
                    far_ref[slot, :, first : first + size], w_ref[...], preferred_element_type=F32
                )
                first += size
            total = total.astype(BF)
            for hi in range(2):
                out_refs[n * 2 + hi][:, before:] = total[:, hi * part : (hi + 1) * part]
        for e_ref, out in zip(e_refs, out_refs):
            out[:, :before] = e_ref[...]

    return call(
        kernel,
        [jax.ShapeDtypeStruct((both, before + part), BF)] * 4,
        [flags],
        [sums, rows_far, *pieces, *earlier, *events],
        limit=8,
        spec=[VMEM_SPEC] * (2 + count + kept) + [ANY_SPEC] * len(events),
        out_spec=VMEM_SPEC,
    )


def attend(flags, guide, queries, caches, q_spec=VMEM_SPEC):
    count, kept = len(queries), len(caches)
    rows, width = queries[0].shape[0] // 2, queries[0].shape[1]
    heads = width // HD
    scale = 1.0 / math.sqrt(HD)
    sizes = [c.shape[0] * c.shape[3] for c in caches]
    firsts = [sum(sizes[:i]) for i in range(kept)]
    keys_all = sum(sizes)
    step = 32 * 1024 // keys_all
    places = [(b, head) for b in range(2) for head in range(heads // 2 * 2)]
    places += [(b, head) for head in range(heads // 2 * 2, heads) for b in range(2)]

    def kernel(s_ref, g_ref, *refs):
        q_refs, c_refs = refs[:count], refs[count : count + kept]
        out, q_buf, two_buf, s_buf, w_buf, sem = refs[-6:]
        for r in range(count):

            @pl.when(s_ref[2] == r)
            def _():
                if q_spec is VMEM_SPEC:
                    q_buf[...] = q_refs[r][...]
                else:
                    pltpu.make_async_copy(q_refs[r], q_buf, sem).start()

        if q_spec is not VMEM_SPEC:
            pltpu.make_async_copy(q_refs[0], q_buf, sem).wait()
        attended = {}
        for n in range(0, len(places), 2):
            pair = places[n : n + 2]
            (b0, h0), (b1, h1) = pair
            turn = n // 2 % 2
            q0 = q_buf[b0 * rows : (b0 + 1) * rows, h0 * HD : (h0 + 1) * HD]
            q1 = q_buf[b1 * rows : (b1 + 1) * rows, h1 * HD : (h1 + 1) * HD]
            none = jnp.zeros_like(q0)
            q = jnp.concatenate(
                [jnp.concatenate([q0, none], axis=1), jnp.concatenate([none, q1], axis=1)], axis=0
            )

            def sides(c_ref, kind, size, first):
                if b0 == b1:
                    return c_ref[:, kind, b0, :, h0 * HD : (h1 + 1) * HD].reshape(size, 2 * HD)
                here = slice(first, first + size)
                two_buf[kind, here, :HD] = c_ref[:, kind, b0, :, h0 * HD : (h0 + 1) * HD].reshape(size, HD)
                two_buf[kind, here, HD:] = c_ref[:, kind, b1, :, h1 * HD : (h1 + 1) * HD].reshape(size, HD)
                return two_buf[kind, here]

            for c_ref, size, first in zip(c_refs, sizes, firsts):
                s_buf[turn, :, first : first + size] = lax.dot_general(
                    q, sides(c_ref, 0, size, first), (((1,), (1,)), ((), ())), preferred_element_type=F32
                )
            for row in range(0, 2 * rows, step):
                here = slice(row, row + step)
                scores = s_buf[turn, here] * scale
                exps = jnp.exp(scores - jnp.max(scores, axis=-1, keepdims=True))
                over = 1.0 / jnp.sum(exps, axis=-1, keepdims=True)
                w_buf[turn, here] = (exps * over).astype(BF)
            result = jnp.zeros((2 * rows, 2 * HD), F32)
            for c_ref, size, first in zip(c_refs, sizes, firsts):
                result = result + jnp.dot(
                    w_buf[turn, :, first : first + size],
                    sides(c_ref, 1, size, first),
                    preferred_element_type=F32,
                )
            attended[pair[0]] = result[:rows, :HD]
            attended[pair[1]] = result[rows:, HD:]
        for head in range(heads):
            guided = attended[1, head] + g_ref[0] * (attended[0, head] - attended[1, head])
            out[:, head * HD : (head + 1) * HD] = guided.astype(BF)

    return call(
        kernel,
        jax.ShapeDtypeStruct((rows, width), BF),
        [flags, guide],
        [*queries, *caches],
        [
            pltpu.VMEM((2 * rows, width), BF),
            pltpu.VMEM((2, keys_all, 2 * HD), BF),
            pltpu.VMEM((2, 2 * rows, keys_all), F32),
            pltpu.VMEM((2, 2 * rows, keys_all), BF),
            pltpu.SemaphoreType.DMA,
        ],
        limit=6 + 8 * (keys_all // 1024),
        spec=[q_spec] * count + [VMEM_SPEC] * kept,
        out_spec=VMEM_SPEC,
    )


def paste(flags, previous, mine, others):
    rows, columns = previous.shape
    width = columns // GROUPS

    def kernel(s_ref, prev_ref, *refs):
        out, sem = refs[-2:]

        def place(m):
            return out.at[:, pl.ds(pl.multiple_of((s_ref[1] ^ m) * width, HD), width)]

        taken = s_ref[3]
        for n in range(len(others)):
            taken = taken + s_ref[4 + n]

        @pl.when(taken == 0)
        def _():
            run_all([pltpu.make_async_copy(prev_ref, out, sem.at[0])])

        @pl.when(s_ref[3] == 1)
        def _():
            run_all([pltpu.make_async_copy(refs[m], place(m), sem.at[m]) for m in range(GROUPS)])

        for n in range(len(others)):

            @pl.when(s_ref[4 + n] == 1)
            def _():
                run_all(
                    [
                        pltpu.make_async_copy(refs[GROUPS * (1 + n) + m], place(m), sem.at[m])
                        for m in range(GROUPS)
                    ]
                )

    return call(
        kernel,
        jax.ShapeDtypeStruct((rows, columns), BF),
        [flags],
        [previous, *mine, *[piece for other in others for piece in other]],
        [pltpu.SemaphoreType.DMA((GROUPS,))],
        spec=VMEM_SPEC,
    )


def body(hidden, key_cache, value_cache, cached_out, w_query, guide, masked_tiles, mask_count):
    images = lax.axis_size("image")
    tokens = lax.axis_size("token")
    heads = key_cache.shape[3] // HD
    per_group = heads // GROUPS
    slots = masked_tiles.shape[1]
    layers = tokens // (2 * GROUPS)
    assert images == 4 and hidden.shape[1] == 1 and hidden.shape[2] == TILE
    assert tokens == layers * 2 * GROUPS and slots == 2 * layers and heads == per_group * GROUPS

    image = lax.axis_index("image")
    token = lax.axis_index("token")
    core = token % 2
    chip = token // 2
    z = chip // layers
    layer = chip % layers
    tiles = masked_tiles[0]

    def over_image(x, m):
        return lax.ppermute(x, "image", [(i, i ^ m) for i in range(images)])

    def over_z(x, m):
        span = 2 * layers
        return lax.ppermute(x, "token", [(t, ((t // span) ^ m) * span + t % span) for t in range(tokens)])

    def over_core(x):
        return lax.ppermute(x, "token", [(t, t ^ 1) for t in range(tokens)])

    def send(x, pairs):
        return lax.ppermute(x, "token", pairs)

    layer_groups = [
        [(s * layers + at) * 2 + c for at in range(layers)] for s in range(GROUPS) for c in range(2)
    ]
    group_groups = [list(range(s * layers * 2, (s + 1) * layers * 2)) for s in range(GROUPS)]
    z_groups = [[s * 2 * layers + at for s in range(GROUPS)] for at in range(2 * layers)]

    plan = [list(range(per_group - 1)), [per_group - 1]]

    def part_heads(k):
        return lambda c: [(2 * c + hi) * per_group + head for hi in range(2) for head in plan[k]]

    half = w_query.shape[0] // 2
    own_hidden = hidden[:, 0]
    other_hidden = over_core(own_hidden)

    in_use = jnp.arange(slots, dtype=jnp.int32) < mask_count[0]
    hit = ((tiles == token) & in_use).astype(jnp.int32)
    my_slot = layer * 2 + core
    other_hits = hit[1 - core][None] if layers == 1 else jnp.where(jnp.arange(slots) == my_slot, 0, hit)
    is_own = (tiles % 2 == core).astype(jnp.int32)
    if layers == 1:
        owners = [tiles[0] // 2, tiles[1] // 2]
        second = jnp.where(mask_count[0] > 1, owners[1], jnp.where(owners[0] < GROUPS // 2, GROUPS - 1, 0))
        which = owners[0] * GROUPS + second
        slot_first = (z != owners[0]).astype(jnp.int32)
        choice = z % 2
        extra = jnp.stack([slot_first, which]).astype(jnp.int32)
    else:
        choice = 0
        extra = jnp.zeros((2,), jnp.int32)
    flags = jnp.concatenate(
        [jnp.stack([image, z, choice, hit[my_slot]]).astype(jnp.int32), other_hits, is_own, extra]
    )
    pairs_from = 4 + other_hits.shape[0]
    first_at = pairs_from + slots

    def near(k, *events):
        own = pack_weights(core[None], w_query, part_heads(k), events)
        return [own, over_image(own, 1), over_image(own, 2)]

    def far(k, *events):
        first, last = halves(flags, weights[k][1], weights[k][2], events)
        return [over_image(first, 2), over_image(last, 1)], first

    def begin(k, *events):
        return [
            begin_project(
                flags, pairs_from + 2 * at, own_hidden, other_hidden, weights[k], w_query.shape[0], events
            )
            for at in range(layers)
        ]

    def finish(at, *events):
        first = finish_project(flags, first_at, *begun_0[at], far_0, events=events)
        return finish_project(flags, first_at, *begun_1[at], far_1, first)

    weights = [near(0)]
    blocks = pack_caches(key_cache[:, 0], value_cache[:, 0], weights[0][:1])
    gathered = lax.all_to_all(blocks, "token", 0, 0, axis_index_groups=z_groups)
    weights.append(near(1, blocks))
    far_0, event = far(0, weights[1][0])
    begun_0 = begin(0, event)
    far_1, event = far(1, begun_0[0][1])
    begun_1 = begin(1, event)

    if layers == 1:
        sent = finish(0, begun_1[0][1])
        gathered = after(gathered, sent[0])
        caches = [gathered, over_core(gathered)]

        def ask(first, second):
            def spread(x, hi, chips):
                return send(
                    x, [(2 * chips[slot] + c, 2 * (2 * c + hi) + slot) for slot in range(2) for c in range(2)]
                )

            def branch(sent):
                if first != second:
                    return [spread(sent[hi], hi, (first, second)) for hi in range(2)]
                far_end = GROUPS - 1 if first < GROUPS // 2 else 0
                for_first = [spread(sent[hi], hi, (first, far_end)) for hi in range(2)]
                for_second = [spread(sent[2 + hi], hi, (far_end, first)) for hi in range(2)]
                return [jnp.where(core == 0, a, b) for a, b in zip(for_first, for_second)]

            return branch

        branches = [ask(a, b) for a in range(GROUPS) for b in range(GROUPS)]
        queries = lax.switch(which, branches, sent)
    else:
        queries = None
        for at in range(layers):
            sent = finish(at, begun_1[at][1])
            sent = jnp.stack([sent[0], sent[2], sent[1], sent[3]])
            came = []
            for r in range(4):
                pairs = []
                for t in range(tokens):
                    c, here, s = t % 2, (t // 2) % layers, t // 2 // layers
                    goal = (s + r) % 4
                    pairs.append((t, ((2 * c + goal // 2) * layers + here) * 2 + goal % 2))
                came.append(send(sent[(z + r) % 4], pairs))
            slot = 2 * at + core
            choice = (2 * (z % 2) + core - tiles[slot] // 2 // layers) % 4
            holds = (tiles[slot] // 2) % layers == layer
            came = jnp.where(holds, jnp.stack(came)[choice], jnp.zeros_like(came[0]))
            came = lax.psum(came, "token", axis_index_groups=layer_groups)
            queries = came if queries is None else jnp.where(layer == at, came, queries)
        queries = [queries]
        everyone = lax.all_gather(gathered, "token", axis_index_groups=group_groups)
        caches = [everyone.reshape(-1, *gathered.shape[1:])]

    guided = attend(flags, guide, queries, caches, ANY_SPEC)
    mine = [guided] + [over_z(guided, m) for m in range(1, GROUPS)]
    if layers == 1:
        others = [[over_core(piece) for piece in mine]]
    else:
        everyone = [lax.all_gather(piece, "token", axis_index_groups=group_groups) for piece in mine]
        others = [[pieces[n] for pieces in everyone] for n in range(slots)]
    return paste(flags, cached_out[0], mine, others)[None]


def solution(mesh):
    return jax.shard_map(
        body,
        mesh=mesh,
        in_specs=(
            P(None, "image", "token", None),
            P(None, "image", "token", None),
            P(None, "image", "token", None),
            P("image", "token", None),
            P("image", None),
            P("image"),
            P("image", None),
            P("image"),
        ),
        out_specs=P("image", "token", None),
        check_vma=False,
    )
```

```python
import math

import jax
import jax.numpy as jnp
from jax import lax
from jax.experimental import pallas as pl
from jax.experimental.pallas import tpu as pltpu
from jax.sharding import PartitionSpec as P

HD = 128
TILE = 128
GROUPS = 4
BF = jnp.bfloat16
F32 = jnp.float32
MIB = 1024 * 1024

SMEM_SPEC = pl.BlockSpec(memory_space=pltpu.SMEM)
ANY_SPEC = pl.BlockSpec(memory_space=pl.ANY)
VMEM_SPEC = pl.BlockSpec(memory_space=pltpu.VMEM)


def call(kernel, out_shape, scalars, arrays, scratch=(), limit=4, aliases=None, spec=ANY_SPEC, out_spec=ANY_SPEC, flops=0):
    many = isinstance(out_shape, (list, tuple))
    return pl.pallas_call(
        kernel,
        out_shape=out_shape,
        in_specs=[SMEM_SPEC] * len(scalars) + (spec if isinstance(spec, list) else [spec] * len(arrays)),
        out_specs=[out_spec] * len(out_shape) if many else out_spec,
        scratch_shapes=list(scratch),
        input_output_aliases=aliases or {},
        compiler_params=pltpu.CompilerParams(vmem_limit_bytes=limit * MIB),
        cost_estimate=pl.CostEstimate(flops=flops, bytes_accessed=0, transcendentals=0),
    )(*scalars, *arrays)


def stays(x):
    return pltpu.with_memory_space_constraint(x, pltpu.HBM)


def run_all(copies):
    for copy in copies:
        copy.start()
    for copy in copies:
        copy.wait()


def run_both(loads, stores):
    for load in loads:
        load.start()
    for load, store in zip(loads, stores):
        load.wait()
        store.start()
    for store in stores:
        store.wait()


def after(x, *events):
    def kernel(*refs):
        pass

    return call(kernel, jax.ShapeDtypeStruct(x.shape, x.dtype), [], [x, *events], aliases={0: 0})


def pack_weights(core, w_query, heads_of, events=()):
    rows, columns = w_query.shape
    count = len(heads_of(0))
    shape = (rows, count * HD)

    def kernel(core_ref, w_ref, *refs):
        out, sem = refs[-2:]
        run_all(
            [
                pltpu.make_async_copy(
                    w_ref.at[:, pl.ds(pl.multiple_of(head * HD, HD), HD)],
                    out.at[:, n * HD : (n + 1) * HD],
                    sem.at[n],
                )
                for n, head in enumerate(heads_of(core_ref[0]))
            ]
        )

    return call(
        kernel,
        jax.ShapeDtypeStruct(shape, BF),
        [core],
        [stays(w_query), *events],
        [pltpu.SemaphoreType.DMA((count,))],
        out_spec=VMEM_SPEC,
    )


def pack_caches(key_block, value_block, events=()):
    branches, tokens, columns = key_block.shape
    width = columns // GROUPS

    def kernel(k_ref, v_ref, *refs):
        out, buf, sem, out_sem = refs[-4:]
        loads, stores = [], []
        for n, ref in enumerate((k_ref, v_ref)):
            for g in range(GROUPS):
                here = buf.at[g, n]
                loads.append(
                    pltpu.make_async_copy(
                        ref.at[:, :, g * width : (g + 1) * width], here, sem.at[n * GROUPS + g]
                    )
                )
                stores.append(pltpu.make_async_copy(here, out.at[g, n], out_sem.at[n * GROUPS + g]))
        run_both(loads, stores)

    shape = (GROUPS, 2, branches, tokens, width)
    return call(
        kernel,
        jax.ShapeDtypeStruct(shape, BF),
        [],
        [stays(key_block), stays(value_block), *events],
        [pltpu.VMEM(shape, BF), pltpu.SemaphoreType.DMA((2 * GROUPS,)), pltpu.SemaphoreType.DMA((2 * GROUPS,))],
    )


def halves(flags, by_x, by_y, events=()):
    rows, width = by_x.shape
    half = rows // 2

    def kernel(_, x_ref, y_ref, *refs):
        first, last, sem = refs[-3:]
        run_all(
            [
                pltpu.make_async_copy(x_ref.at[:half], first, sem.at[0]),
                pltpu.make_async_copy(y_ref.at[half:], last, sem.at[1]),
            ]
        )

    return call(
        kernel,
        [jax.ShapeDtypeStruct((half, width), BF)] * 2,
        [flags],
        [by_x, by_y, *events],
        [pltpu.SemaphoreType.DMA((2,))],
        out_spec=VMEM_SPEC,
    )


def begin_project(flags, at, core_at, own, other, w_query, heads_of, pieces, far_rows, events=()):
    branches, rows, depth = own.shape
    chunk, width = pieces[0].shape
    count = 1 + len(pieces)
    both = branches * rows

    def kernel(s_ref, own_ref, other_ref, w_ref, *refs):
        t_ref, far_ref, h_buf, w_buf, sem, w_sem = refs[-6:]
        loads = []
        for n in range(count + 1):
            columns = pl.ds(pl.multiple_of((s_ref[0] ^ n) * chunk, HD), chunk)
            loads.append([])
            if n == 0:
                for k, head in enumerate(heads_of(s_ref[core_at])):
                    columns_of = pl.ds(pl.multiple_of(head * HD, HD), HD)
                    loads[n].append(
                        pltpu.make_async_copy(
                            w_ref.at[:, columns_of], w_buf.at[n, :, k * HD : (k + 1) * HD], w_sem.at[k]
                        )
                    )
                    loads[n][k].start()
            elif n < count:
                loads[n].append(pltpu.make_async_copy(refs[n - 1], w_buf.at[n], w_sem.at[width // HD + n]))
                loads[n][0].start()
            for slot in range(2):
                for b in range(branches):
                    there = h_buf.at[n, slot] if n < count else far_ref.at[slot]
                    there = there.at[b * rows : (b + 1) * rows]
                    mine, theirs = [
                        pltpu.make_async_copy(ref.at[b, :, columns], there, sem.at[n, slot, b])
                        for ref in (own_ref, other_ref)
                    ]
                    loads[n].append(mine)

                    @pl.when(s_ref[at + slot] == 1)
                    def _():
                        mine.start()

                    @pl.when(s_ref[at + slot] != 1)
                    def _():
                        theirs.start()

        for n in range(count):
            for load in loads[n]:
                load.wait()
            for slot in range(2):
                product = jnp.dot(h_buf[n, slot], w_buf[n], preferred_element_type=F32)
                if n == 0:
                    t_ref[slot] = product
                else:
                    t_ref[slot] += product
        for load in loads[count]:
            load.wait()

    return call(
        kernel,
        [jax.ShapeDtypeStruct((2, both, width), F32), jax.ShapeDtypeStruct((2, both, far_rows), BF)],
        [flags],
        [own, other, stays(w_query), *pieces, *events],
        [
            pltpu.VMEM((count, 2, both, chunk), BF),
            pltpu.VMEM((count, chunk, width), BF),
            pltpu.SemaphoreType.DMA((count + 1, 2, branches)),
            pltpu.SemaphoreType.DMA((width // HD + count,)),
        ],
        limit=16,
        out_spec=VMEM_SPEC,
        flops=25_000_000_000,
    )


def finish_project(flags, first_at, sums, rows_far, pieces, earlier=(), events=()):
    _, both, width = sums.shape
    part = width // 2
    count, kept = len(pieces), len(earlier)
    before = earlier[0].shape[1] if earlier else 0

    def kernel(s_ref, t_ref, far_ref, *refs):
        w_refs, e_refs, out_refs = refs[:count], refs[count : count + kept], refs[-4:]

        def make(n, slot):
            total, first = t_ref[slot], 0
            for w_ref in w_refs:
                size = w_ref.shape[0]
                total = total + jnp.dot(
                    far_ref[slot, :, first : first + size], w_ref[...], preferred_element_type=F32
                )
                first += size
            total = total.astype(BF)
            for hi in range(2):
                out = out_refs[n * 2 + hi]
                out[:, before:] = total[:, hi * part : (hi + 1) * part]
                if e_refs:
                    out[:, :before] = e_refs[n * 2 + hi][...]

        make(0, s_ref[first_at])

        @pl.when(s_ref[first_at + 3] == 1)
        def _():
            make(1, 1)

    return call(
        kernel,
        [jax.ShapeDtypeStruct((both, before + part), BF)] * 4,
        [flags],
        [sums, rows_far, *pieces, *earlier, *events],
        limit=8,
        spec=[VMEM_SPEC] * (2 + count + kept) + [ANY_SPEC] * len(events),
        out_spec=VMEM_SPEC,
    )


def attend(flags, guide, queries, caches, q_spec=VMEM_SPEC):
    count, kept = len(queries), len(caches)
    rows, width = queries[0].shape[0] // 2, queries[0].shape[1]
    heads = width // HD
    scale = 1.0 / math.sqrt(HD)
    sizes = [c.shape[0] * c.shape[3] for c in caches]
    firsts = [sum(sizes[:i]) for i in range(kept)]
    keys_all = sum(sizes)
    step = 32 * 1024 // keys_all
    places = [(b, head) for b in range(2) for head in range(heads // 2 * 2)]
    places += [(b, head) for head in range(heads // 2 * 2, heads) for b in range(2)]
    assert heads == 3

    def kernel(s_ref, g_ref, *refs):
        q_refs, c_refs = refs[:count], refs[count : count + kept]
        out, q_buf, two_buf, s_buf, w_buf, sem = refs[-6:]
        for r in range(count):

            @pl.when(s_ref[2] == r)
            def _():
                if q_spec is VMEM_SPEC:
                    q_buf[...] = q_refs[r][...]
                else:
                    pltpu.make_async_copy(q_refs[r], q_buf, sem).start()

        for b, head in places[2 * (heads // 2 * 2) :]:
            for c_ref, size, first in zip(c_refs, sizes, firsts):
                for kind in range(2):
                    two_buf[kind, first : first + size, b * HD : (b + 1) * HD] = c_ref[
                        :, kind, b, :, head * HD : (head + 1) * HD
                    ].reshape(size, HD)
        if q_spec is not VMEM_SPEC:
            pltpu.make_async_copy(q_refs[0], q_buf, sem).wait()
        attended = {}
        for n in range(0, len(places), 2):
            pair = places[n : n + 2]
            (b0, h0), (b1, h1) = pair
            turn = n // 2 % 2
            q0 = q_buf[b0 * rows : (b0 + 1) * rows, h0 * HD : (h0 + 1) * HD]
            q1 = q_buf[b1 * rows : (b1 + 1) * rows, h1 * HD : (h1 + 1) * HD]
            none = jnp.zeros_like(q0)
            q = jnp.concatenate(
                [jnp.concatenate([q0, none], axis=1), jnp.concatenate([none, q1], axis=1)], axis=0
            )

            def sides(c_ref, kind, size, first):
                if b0 == b1:
                    return c_ref[:, kind, b0, :, h0 * HD : (h1 + 1) * HD].reshape(size, 2 * HD)
                return two_buf[kind, first : first + size]

            for c_ref, size, first in zip(c_refs, sizes, firsts):
                s_buf[turn, :, first : first + size] = lax.dot_general(
                    q, sides(c_ref, 0, size, first), (((1,), (1,)), ((), ())), preferred_element_type=F32
                )
            for row in range(0, 2 * rows, step):
                here = slice(row, row + step)
                scores = s_buf[turn, here] * scale
                exps = jnp.exp(scores - jnp.max(scores, axis=-1, keepdims=True))
                over = 1.0 / jnp.sum(exps, axis=-1, keepdims=True)
                w_buf[turn, here] = (exps * over).astype(BF)
            result = jnp.zeros((2 * rows, 2 * HD), F32)
            for c_ref, size, first in zip(c_refs, sizes, firsts):
                result = result + jnp.dot(
                    w_buf[turn, :, first : first + size],
                    sides(c_ref, 1, size, first),
                    preferred_element_type=F32,
                )
            attended[pair[0]] = result[:rows, :HD]
            attended[pair[1]] = result[rows:, HD:]
        for head in range(heads):
            guided = attended[1, head] + g_ref[0] * (attended[0, head] - attended[1, head])
            out[:, head * HD : (head + 1) * HD] = guided.astype(BF)

    return call(
        kernel,
        jax.ShapeDtypeStruct((rows, width), BF),
        [flags, guide],
        [*queries, *caches],
        [
            pltpu.VMEM((2 * rows, width), BF),
            pltpu.VMEM((2, keys_all, 2 * HD), BF),
            pltpu.VMEM((2, 2 * rows, keys_all), F32),
            pltpu.VMEM((2, 2 * rows, keys_all), BF),
            pltpu.SemaphoreType.DMA,
        ],
        limit=6 + 8 * (keys_all // 1024),
        spec=[q_spec] * count + [VMEM_SPEC] * kept,
        out_spec=VMEM_SPEC,
    )


def paste(flags, previous, mine, others):
    rows, columns = previous.shape
    width = columns // GROUPS

    def kernel(s_ref, prev_ref, *refs):
        out, sem = refs[-2:]

        def place(m):
            return out.at[:, pl.ds(pl.multiple_of((s_ref[1] ^ m) * width, HD), width)]

        taken = s_ref[3]
        for n in range(len(others)):
            taken = taken + s_ref[4 + n]

        @pl.when(taken == 0)
        def _():
            run_all([pltpu.make_async_copy(prev_ref, out, sem.at[0])])

        @pl.when(s_ref[3] == 1)
        def _():
            run_all([pltpu.make_async_copy(refs[m], place(m), sem.at[m]) for m in range(GROUPS)])

        for n in range(len(others)):

            @pl.when(s_ref[4 + n] == 1)
            def _():
                run_all(
                    [
                        pltpu.make_async_copy(refs[GROUPS * (1 + n) + m], place(m), sem.at[m])
                        for m in range(GROUPS)
                    ]
                )

    return call(
        kernel,
        jax.ShapeDtypeStruct((rows, columns), BF),
        [flags],
        [previous, *mine, *[piece for other in others for piece in other]],
        [pltpu.SemaphoreType.DMA((GROUPS,))],
        spec=VMEM_SPEC,
    )


def body(hidden, key_cache, value_cache, cached_out, w_query, guide, masked_tiles, mask_count):
    images = lax.axis_size("image")
    tokens = lax.axis_size("token")
    heads = key_cache.shape[3] // HD
    per_group = heads // GROUPS
    slots = masked_tiles.shape[1]
    layers = tokens // (2 * GROUPS)
    assert images == 4 and hidden.shape[1] == 1 and hidden.shape[2] == TILE
    assert tokens == layers * 2 * GROUPS and slots == 2 * layers and heads == per_group * GROUPS

    image = lax.axis_index("image")
    token = lax.axis_index("token")
    core = token % 2
    chip = token // 2
    z = chip // layers
    layer = chip % layers
    tiles = masked_tiles[0]

    def over_image(x, m):
        return lax.ppermute(x, "image", [(i, i ^ m) for i in range(images)])

    def over_z(x, m):
        span = 2 * layers
        return lax.ppermute(x, "token", [(t, ((t // span) ^ m) * span + t % span) for t in range(tokens)])

    def over_core(x):
        return lax.ppermute(x, "token", [(t, t ^ 1) for t in range(tokens)])

    def send(x, pairs):
        return lax.ppermute(x, "token", pairs)

    layer_groups = [
        [(s * layers + at) * 2 + c for at in range(layers)] for s in range(GROUPS) for c in range(2)
    ]
    group_groups = [list(range(s * layers * 2, (s + 1) * layers * 2)) for s in range(GROUPS)]
    z_groups = [[s * 2 * layers + at for s in range(GROUPS)] for at in range(2 * layers)]

    plan = [list(range(per_group - 1)), [per_group - 1]]

    def part_heads(k):
        return lambda c: [(2 * c + hi) * per_group + head for hi in range(2) for head in plan[k]]

    half = w_query.shape[0] // 2
    own_hidden = hidden[:, 0]
    other_hidden = over_core(own_hidden)

    in_use = jnp.arange(slots, dtype=jnp.int32) < mask_count[0]
    hit = ((tiles == token) & in_use).astype(jnp.int32)
    my_slot = layer * 2 + core
    other_hits = hit[1 - core][None] if layers == 1 else jnp.where(jnp.arange(slots) == my_slot, 0, hit)
    is_own = (tiles % 2 == core).astype(jnp.int32)
    if layers == 1:
        owners = [tiles[0] // 2, tiles[1] // 2]
        second = jnp.where(mask_count[0] > 1, owners[1], jnp.where(owners[0] < GROUPS // 2, GROUPS - 1, 0))
        which = owners[0] * GROUPS + second
        slot_first = (z != owners[0]).astype(jnp.int32)
        choice = z % 2
        shared = owners[0] == second
        extra = jnp.stack([slot_first, which, core, shared]).astype(jnp.int32)
    else:
        choice = 0
        extra = jnp.stack([0, 0, core, 1]).astype(jnp.int32)
    flags = jnp.concatenate(
        [jnp.stack([image, z, choice, hit[my_slot]]).astype(jnp.int32), other_hits, is_own, extra]
    )
    pairs_from = 4 + other_hits.shape[0]
    first_at = pairs_from + slots

    def near(k, *events):
        own = pack_weights(core[None], w_query, part_heads(k), events)
        return [own, over_image(own, 1), over_image(own, 2)]

    def far(k, *events):
        first, last = halves(flags, weights[k][1], weights[k][2], events)
        return [over_image(first, 2), over_image(last, 1)], first

    def begin(k, *events):
        return [
            begin_project(
                flags,
                pairs_from + 2 * at,
                first_at + 2,
                own_hidden,
                other_hidden,
                w_query,
                part_heads(k),
                weights[k][1:],
                w_query.shape[0],
                events,
            )
            for at in range(layers)
        ]

    def finish(at, *events):
        first = finish_project(flags, first_at, *begun_0[at], far_0, events=events)
        return finish_project(flags, first_at, *begun_1[at], far_1, first)

    weights = [near(0)]
    blocks = pack_caches(key_cache[:, 0], value_cache[:, 0], weights[0][:1])
    gathered = lax.all_to_all(blocks, "token", 0, 0, axis_index_groups=z_groups)
    weights.append(near(1, blocks))
    far_0, event = far(0, weights[1][0])
    begun_0 = begin(0, event)
    far_1, event = far(1, begun_0[0][1])
    begun_1 = begin(1, event)

    if layers == 1:
        sent = finish(0, begun_1[0][1])
        gathered = after(gathered, sent[0])
        caches = [gathered, over_core(gathered)]

        def ask(first, second):
            def spread(x, hi, chips):
                return send(
                    x, [(2 * chips[slot] + c, 2 * (2 * c + hi) + slot) for slot in range(2) for c in range(2)]
                )

            def branch(sent):
                if first != second:
                    return [spread(sent[hi], hi, (first, second)) for hi in range(2)]
                far_end = GROUPS - 1 if first < GROUPS // 2 else 0
                for_first = [spread(sent[hi], hi, (first, far_end)) for hi in range(2)]
                for_second = [spread(sent[2 + hi], hi, (far_end, first)) for hi in range(2)]
                return [jnp.where(core == 0, a, b) for a, b in zip(for_first, for_second)]

            return branch

        branches = [ask(a, b) for a in range(GROUPS) for b in range(GROUPS)]
        queries = lax.switch(which, branches, sent)
    else:
        queries = None
        for at in range(layers):
            sent = finish(at, begun_1[at][1])
            sent = jnp.stack([sent[0], sent[2], sent[1], sent[3]])
            came = []
            for r in range(4):
                pairs = []
                for t in range(tokens):
                    c, here, s = t % 2, (t // 2) % layers, t // 2 // layers
                    goal = (s + r) % 4
                    pairs.append((t, ((2 * c + goal // 2) * layers + here) * 2 + goal % 2))
                came.append(send(sent[(z + r) % 4], pairs))
            slot = 2 * at + core
            choice = (2 * (z % 2) + core - tiles[slot] // 2 // layers) % 4
            holds = (tiles[slot] // 2) % layers == layer
            came = jnp.where(holds, jnp.stack(came)[choice], jnp.zeros_like(came[0]))
            came = lax.psum(came, "token", axis_index_groups=layer_groups)
            queries = came if queries is None else jnp.where(layer == at, came, queries)
        queries = [queries]
        everyone = lax.all_gather(gathered, "token", axis_index_groups=group_groups)
        caches = [everyone.reshape(-1, *gathered.shape[1:])]

    guided = attend(flags, guide, queries, caches, ANY_SPEC)
    mine = [guided] + [over_z(guided, m) for m in range(1, GROUPS)]
    if layers == 1:
        others = [[over_core(piece) for piece in mine]]
    else:
        everyone = [lax.all_gather(piece, "token", axis_index_groups=group_groups) for piece in mine]
        others = [[pieces[n] for pieces in everyone] for n in range(slots)]
    return paste(flags, cached_out[0], mine, others)[None]


def solution(mesh):
    return jax.shard_map(
        body,
        mesh=mesh,
        in_specs=(
            P(None, "image", "token", None),
            P(None, "image", "token", None),
            P(None, "image", "token", None),
            P("image", "token", None),
            P("image", None),
            P("image"),
            P("image", None),
            P("image"),
        ),
        out_specs=P("image", "token", None),
        check_vma=False,
    )
```

```python
import math

import jax
import jax.numpy as jnp
from jax import lax
from jax.experimental import pallas as pl
from jax.experimental.pallas import tpu as pltpu
from jax.sharding import PartitionSpec as P

HD = 128
TILE = 128
GROUPS = 4
BF = jnp.bfloat16
F32 = jnp.float32
MIB = 1024 * 1024

SMEM_SPEC = pl.BlockSpec(memory_space=pltpu.SMEM)
ANY_SPEC = pl.BlockSpec(memory_space=pl.ANY)
VMEM_SPEC = pl.BlockSpec(memory_space=pltpu.VMEM)


def call(kernel, out_shape, scalars, arrays, scratch=(), limit=4, aliases=None, spec=ANY_SPEC, out_spec=ANY_SPEC, flops=0):
    many = isinstance(out_shape, (list, tuple))
    return pl.pallas_call(
        kernel,
        out_shape=out_shape,
        in_specs=[SMEM_SPEC] * len(scalars) + (spec if isinstance(spec, list) else [spec] * len(arrays)),
        out_specs=[out_spec] * len(out_shape) if many else out_spec,
        scratch_shapes=list(scratch),
        input_output_aliases=aliases or {},
        compiler_params=pltpu.CompilerParams(vmem_limit_bytes=limit * MIB),
        cost_estimate=pl.CostEstimate(flops=flops, bytes_accessed=0, transcendentals=0),
    )(*scalars, *arrays)


def stays(x):
    return pltpu.with_memory_space_constraint(x, pltpu.HBM)


def run_all(copies):
    for copy in copies:
        copy.start()
    for copy in copies:
        copy.wait()


def run_both(loads, stores):
    for load in loads:
        load.start()
    for load, store in zip(loads, stores):
        load.wait()
        store.start()
    for store in stores:
        store.wait()


def after(x, *events):
    def kernel(*refs):
        pass

    return call(kernel, jax.ShapeDtypeStruct(x.shape, x.dtype), [], [x, *events], aliases={0: 0})


def pack_weights(core, w_query, heads_of, events=()):
    rows, columns = w_query.shape
    count = len(heads_of(0))
    shape = (rows, count * HD)

    def kernel(core_ref, w_ref, *refs):
        out, sem = refs[-2:]
        run_all(
            [
                pltpu.make_async_copy(
                    w_ref.at[:, pl.ds(pl.multiple_of(head * HD, HD), HD)],
                    out.at[:, n * HD : (n + 1) * HD],
                    sem.at[n],
                )
                for n, head in enumerate(heads_of(core_ref[0]))
            ]
        )

    return call(
        kernel,
        jax.ShapeDtypeStruct(shape, BF),
        [core],
        [stays(w_query), *events],
        [pltpu.SemaphoreType.DMA((count,))],
        out_spec=VMEM_SPEC,
    )


def pack_caches(key_block, value_block, events=()):
    branches, tokens, columns = key_block.shape
    width = columns // GROUPS

    def kernel(k_ref, v_ref, *refs):
        out, buf, sem, out_sem = refs[-4:]
        loads, stores = [], []
        for n, ref in enumerate((k_ref, v_ref)):
            for g in range(GROUPS):
                here = buf.at[g, n]
                loads.append(
                    pltpu.make_async_copy(
                        ref.at[:, :, g * width : (g + 1) * width], here, sem.at[n * GROUPS + g]
                    )
                )
                stores.append(pltpu.make_async_copy(here, out.at[g, n], out_sem.at[n * GROUPS + g]))
        run_both(loads, stores)

    shape = (GROUPS, 2, branches, tokens, width)
    return call(
        kernel,
        jax.ShapeDtypeStruct(shape, BF),
        [],
        [stays(key_block), stays(value_block), *events],
        [pltpu.VMEM(shape, BF), pltpu.SemaphoreType.DMA((2 * GROUPS,)), pltpu.SemaphoreType.DMA((2 * GROUPS,))],
    )


def halves(flags, guide, by_x, by_y, events=()):
    rows, width = by_x.shape
    half = rows // 2

    def kernel(_, __, x_ref, y_ref, *refs):
        first, last, sem = refs[-3:]
        run_all(
            [
                pltpu.make_async_copy(x_ref.at[:half], first, sem.at[0]),
                pltpu.make_async_copy(y_ref.at[half:], last, sem.at[1]),
            ]
        )

    return call(
        kernel,
        [jax.ShapeDtypeStruct((half, width), BF)] * 2,
        [flags, guide],
        [by_x, by_y, *events],
        [pltpu.SemaphoreType.DMA((2,))],
        out_spec=VMEM_SPEC,
    )


def begin_project(flags, at, core_at, own, other, w_query, heads_of, pieces, far_rows, events=()):
    branches, rows, depth = own.shape
    chunk, width = pieces[0].shape
    count = 1 + len(pieces)
    both = branches * rows

    def kernel(s_ref, own_ref, other_ref, w_ref, *refs):
        t_ref, far_ref, h_buf, w_buf, sem, w_sem = refs[-6:]
        loads = []
        for n in range(count + 1):
            columns = pl.ds(pl.multiple_of((s_ref[0] ^ n) * chunk, HD), chunk)
            loads.append([])
            if n == 0:
                for k, head in enumerate(heads_of(s_ref[core_at])):
                    columns_of = pl.ds(pl.multiple_of(head * HD, HD), HD)
                    loads[n].append(
                        pltpu.make_async_copy(
                            w_ref.at[:, columns_of], w_buf.at[n, :, k * HD : (k + 1) * HD], w_sem.at[k]
                        )
                    )
                    loads[n][k].start()
            elif n < count:
                loads[n].append(pltpu.make_async_copy(refs[n - 1], w_buf.at[n], w_sem.at[width // HD + n]))
                loads[n][0].start()
            for slot in range(2):
                for b in range(branches):
                    there = h_buf.at[n, slot] if n < count else far_ref.at[slot]
                    there = there.at[b * rows : (b + 1) * rows]
                    mine, theirs = [
                        pltpu.make_async_copy(ref.at[b, :, columns], there, sem.at[n, slot, b])
                        for ref in (own_ref, other_ref)
                    ]
                    loads[n].append(mine)

                    @pl.when(s_ref[at + slot] == 1)
                    def _():
                        mine.start()

                    @pl.when(s_ref[at + slot] != 1)
                    def _():
                        theirs.start()

        for n in range(count):
            for load in loads[n]:
                load.wait()
            for slot in range(2):
                product = jnp.dot(h_buf[n, slot], w_buf[n], preferred_element_type=F32)
                if n == 0:
                    t_ref[slot] = product
                else:
                    t_ref[slot] += product
        for load in loads[count]:
            load.wait()

    return call(
        kernel,
        [jax.ShapeDtypeStruct((2, both, width), F32), jax.ShapeDtypeStruct((2, both, far_rows), BF)],
        [flags],
        [own, other, stays(w_query), *pieces, *events],
        [
            pltpu.VMEM((count, 2, both, chunk), BF),
            pltpu.VMEM((count, chunk, width), BF),
            pltpu.SemaphoreType.DMA((count + 1, 2, branches)),
            pltpu.SemaphoreType.DMA((width // HD + count,)),
        ],
        limit=16,
        out_spec=VMEM_SPEC,
        flops=25_000_000_000,
    )


def finish_project(flags, first_at, sums, rows_far, pieces, earlier=(), events=()):
    _, both, width = sums.shape
    part = width // 2
    count, kept = len(pieces), len(earlier)
    before = earlier[0].shape[1] if earlier else 0

    def kernel(s_ref, t_ref, far_ref, *refs):
        w_refs, e_refs, out_refs = refs[:count], refs[count : count + kept], refs[-4:]

        def make(n, slot):
            total, first = t_ref[slot], 0
            for w_ref in w_refs:
                size = w_ref.shape[0]
                total = total + jnp.dot(
                    far_ref[slot, :, first : first + size], w_ref[...], preferred_element_type=F32
                )
                first += size
            total = total.astype(BF)
            for hi in range(2):
                out = out_refs[n * 2 + hi]
                out[:, before:] = total[:, hi * part : (hi + 1) * part]
                if e_refs:
                    out[:, :before] = e_refs[n * 2 + hi][...]

        make(0, s_ref[first_at])

        @pl.when(s_ref[first_at + 3] == 1)
        def _():
            make(1, 1)

    return call(
        kernel,
        [jax.ShapeDtypeStruct((both, before + part), BF)] * 4,
        [flags],
        [sums, rows_far, *pieces, *earlier, *events],
        limit=8,
        spec=[VMEM_SPEC] * (2 + count + kept) + [ANY_SPEC] * len(events),
        out_spec=VMEM_SPEC,
    )


def attend(flags, guide, queries, caches, q_spec=VMEM_SPEC):
    count, kept = len(queries), len(caches)
    rows, width = queries[0].shape[0] // 2, queries[0].shape[1]
    heads = width // HD
    scale = 1.0 / math.sqrt(HD)
    sizes = [c.shape[0] * c.shape[3] for c in caches]
    firsts = [sum(sizes[:i]) for i in range(kept)]
    keys_all = sum(sizes)
    step = 32 * 1024 // keys_all
    places = [(b, head) for b in range(2) for head in range(heads // 2 * 2)]
    places += [(b, head) for head in range(heads // 2 * 2, heads) for b in range(2)]
    assert heads == 3

    def kernel(s_ref, g_ref, *refs):
        q_refs, c_refs = refs[:count], refs[count : count + kept]
        out, q_buf, two_buf, s_buf, w_buf, sem = refs[-6:]
        for r in range(count):

            @pl.when(s_ref[2] == r)
            def _():
                if q_spec is VMEM_SPEC:
                    q_buf[...] = q_refs[r][...]
                else:
                    pltpu.make_async_copy(q_refs[r], q_buf, sem).start()

        for b, head in places[2 * (heads // 2 * 2) :]:
            for c_ref, size, first in zip(c_refs, sizes, firsts):
                for kind in range(2):
                    two_buf[kind, first : first + size, b * HD : (b + 1) * HD] = c_ref[
                        :, kind, b, :, head * HD : (head + 1) * HD
                    ].reshape(size, HD)
        if q_spec is not VMEM_SPEC:
            pltpu.make_async_copy(q_refs[0], q_buf, sem).wait()
        attended = {}
        for n in range(0, len(places), 2):
            pair = places[n : n + 2]
            (b0, h0), (b1, h1) = pair
            turn = n // 2 % 2
            q0 = q_buf[b0 * rows : (b0 + 1) * rows, h0 * HD : (h0 + 1) * HD]
            q1 = q_buf[b1 * rows : (b1 + 1) * rows, h1 * HD : (h1 + 1) * HD]
            none = jnp.zeros_like(q0)
            q = jnp.concatenate(
                [jnp.concatenate([q0, none], axis=1), jnp.concatenate([none, q1], axis=1)], axis=0
            )

            def sides(c_ref, kind, size, first):
                if b0 == b1:
                    return c_ref[:, kind, b0, :, h0 * HD : (h1 + 1) * HD].reshape(size, 2 * HD)
                return two_buf[kind, first : first + size]

            for c_ref, size, first in zip(c_refs, sizes, firsts):
                s_buf[turn, :, first : first + size] = lax.dot_general(
                    q, sides(c_ref, 0, size, first), (((1,), (1,)), ((), ())), preferred_element_type=F32
                )
            for row in range(0, 2 * rows, step):
                here = slice(row, row + step)
                scores = s_buf[turn, here] * scale
                exps = jnp.exp(scores - jnp.max(scores, axis=-1, keepdims=True))
                over = 1.0 / jnp.sum(exps, axis=-1, keepdims=True)
                w_buf[turn, here] = (exps * over).astype(BF)
            result = jnp.zeros((2 * rows, 2 * HD), F32)
            for c_ref, size, first in zip(c_refs, sizes, firsts):
                result = result + jnp.dot(
                    w_buf[turn, :, first : first + size],
                    sides(c_ref, 1, size, first),
                    preferred_element_type=F32,
                )
            attended[pair[0]] = result[:rows, :HD]
            attended[pair[1]] = result[rows:, HD:]
        for head in range(heads):
            guided = attended[1, head] + g_ref[0] * (attended[0, head] - attended[1, head])
            out[:, head * HD : (head + 1) * HD] = guided.astype(BF)

    return call(
        kernel,
        jax.ShapeDtypeStruct((rows, width), BF),
        [flags, guide],
        [*queries, *caches],
        [
            pltpu.VMEM((2 * rows, width), BF),
            pltpu.VMEM((2, keys_all, 2 * HD), BF),
            pltpu.VMEM((2, 2 * rows, keys_all), F32),
            pltpu.VMEM((2, 2 * rows, keys_all), BF),
            pltpu.SemaphoreType.DMA,
        ],
        limit=6 + 8 * (keys_all // 1024),
        spec=[q_spec] * count + [VMEM_SPEC] * kept,
        out_spec=VMEM_SPEC,
    )


def paste(flags, previous, mine, others):
    rows, columns = previous.shape
    width = columns // GROUPS

    def kernel(s_ref, prev_ref, *refs):
        out, sem = refs[-2:]

        def place(m):
            return out.at[:, pl.ds(pl.multiple_of((s_ref[1] ^ m) * width, HD), width)]

        taken = s_ref[3]
        for n in range(len(others)):
            taken = taken + s_ref[4 + n]

        @pl.when(taken == 0)
        def _():
            run_all([pltpu.make_async_copy(prev_ref, out, sem.at[0])])

        @pl.when(s_ref[3] == 1)
        def _():
            run_all([pltpu.make_async_copy(refs[m], place(m), sem.at[m]) for m in range(GROUPS)])

        for n in range(len(others)):

            @pl.when(s_ref[4 + n] == 1)
            def _():
                run_all(
                    [
                        pltpu.make_async_copy(refs[GROUPS * (1 + n) + m], place(m), sem.at[m])
                        for m in range(GROUPS)
                    ]
                )

    return call(
        kernel,
        jax.ShapeDtypeStruct((rows, columns), BF),
        [flags],
        [previous, *mine, *[piece for other in others for piece in other]],
        [pltpu.SemaphoreType.DMA((GROUPS,))],
        spec=VMEM_SPEC,
    )


def body(hidden, key_cache, value_cache, cached_out, w_query, guide, masked_tiles, mask_count):
    images = lax.axis_size("image")
    tokens = lax.axis_size("token")
    heads = key_cache.shape[3] // HD
    per_group = heads // GROUPS
    slots = masked_tiles.shape[1]
    layers = tokens // (2 * GROUPS)
    assert images == 4 and hidden.shape[1] == 1 and hidden.shape[2] == TILE
    assert tokens == layers * 2 * GROUPS and slots == 2 * layers and heads == per_group * GROUPS

    image = lax.axis_index("image")
    token = lax.axis_index("token")
    core = token % 2
    chip = token // 2
    z = chip // layers
    layer = chip % layers
    tiles = masked_tiles[0]

    def over_image(x, m):
        return lax.ppermute(x, "image", [(i, i ^ m) for i in range(images)])

    def over_z(x, m):
        span = 2 * layers
        return lax.ppermute(x, "token", [(t, ((t // span) ^ m) * span + t % span) for t in range(tokens)])

    def over_core(x):
        return lax.ppermute(x, "token", [(t, t ^ 1) for t in range(tokens)])

    def send(x, pairs):
        return lax.ppermute(x, "token", pairs)

    layer_groups = [
        [(s * layers + at) * 2 + c for at in range(layers)] for s in range(GROUPS) for c in range(2)
    ]
    group_groups = [list(range(s * layers * 2, (s + 1) * layers * 2)) for s in range(GROUPS)]
    z_groups = [[s * 2 * layers + at for s in range(GROUPS)] for at in range(2 * layers)]

    plan = [list(range(per_group - 1)), [per_group - 1]]

    def part_heads(k):
        return lambda c: [(2 * c + hi) * per_group + head for hi in range(2) for head in plan[k]]

    half = w_query.shape[0] // 2
    own_hidden = hidden[:, 0]
    other_hidden = over_core(own_hidden)

    in_use = jnp.arange(slots, dtype=jnp.int32) < mask_count[0]
    hit = ((tiles == token) & in_use).astype(jnp.int32)
    my_slot = layer * 2 + core
    other_hits = hit[1 - core][None] if layers == 1 else jnp.where(jnp.arange(slots) == my_slot, 0, hit)
    is_own = (tiles % 2 == core).astype(jnp.int32)
    if layers == 1:
        owners = [tiles[0] // 2, tiles[1] // 2]
        second = jnp.where(mask_count[0] > 1, owners[1], jnp.where(owners[0] < GROUPS // 2, GROUPS - 1, 0))
        which = owners[0] * GROUPS + second
        slot_first = (z != owners[0]).astype(jnp.int32)
        choice = z % 2
        shared = owners[0] == second
        extra = jnp.stack([slot_first, which, core, shared]).astype(jnp.int32)
    else:
        choice = 0
        extra = jnp.stack([0, 0, core, 1]).astype(jnp.int32)
    flags = jnp.concatenate(
        [jnp.stack([image, z, choice, hit[my_slot]]).astype(jnp.int32), other_hits, is_own, extra]
    )
    pairs_from = 4 + other_hits.shape[0]
    first_at = pairs_from + slots

    def near(k, *events):
        own = pack_weights(core[None], w_query, part_heads(k), events)
        return [own, over_image(own, 1), over_image(own, 2)]

    def far(k, *events):
        first, last = halves(flags, guide, weights[k][1], weights[k][2], events)
        return [over_image(first, 2), over_image(last, 1)], first

    def begin(k, *events):
        return [
            begin_project(
                flags,
                pairs_from + 2 * at,
                first_at + 2,
                own_hidden,
                other_hidden,
                w_query,
                part_heads(k),
                weights[k][1:],
                w_query.shape[0],
                events,
            )
            for at in range(layers)
        ]

    def finish(at, *events):
        first = finish_project(flags, first_at, *begun_0[at], far_0, events=events)
        return finish_project(flags, first_at, *begun_1[at], far_1, first)

    weights = [near(0)]
    blocks = pack_caches(key_cache[:, 0], value_cache[:, 0], weights[0][:1])
    gathered = lax.all_to_all(blocks, "token", 0, 0, axis_index_groups=z_groups)
    weights.append(near(1, blocks))
    far_0, event = far(0, weights[1][0])
    begun_0 = begin(0, event)
    far_1, event = far(1, begun_0[0][1])
    begun_1 = begin(1, event)

    if layers == 1:
        sent = finish(0, begun_1[0][1])
        gathered = after(gathered, sent[0])
        caches = [gathered, over_core(gathered)]

        def ask(first, second):
            def spread(x, hi, chips):
                return send(
                    x, [(2 * chips[slot] + c, 2 * (2 * c + hi) + slot) for slot in range(2) for c in range(2)]
                )

            def branch(sent):
                if first != second:
                    return [spread(sent[hi], hi, (first, second)) for hi in range(2)]
                far_end = GROUPS - 1 if first < GROUPS // 2 else 0
                for_first = [spread(sent[hi], hi, (first, far_end)) for hi in range(2)]
                for_second = [spread(sent[2 + hi], hi, (far_end, first)) for hi in range(2)]
                return [jnp.where(core == 0, a, b) for a, b in zip(for_first, for_second)]

            return branch

        branches = [ask(a, b) for a in range(GROUPS) for b in range(GROUPS)]
        queries = lax.switch(which, branches, sent)
    else:
        queries = None
        for at in range(layers):
            sent = finish(at, begun_1[at][1])
            sent = jnp.stack([sent[0], sent[2], sent[1], sent[3]])
            came = []
            for r in range(4):
                pairs = []
                for t in range(tokens):
                    c, here, s = t % 2, (t // 2) % layers, t // 2 // layers
                    goal = (s + r) % 4
                    pairs.append((t, ((2 * c + goal // 2) * layers + here) * 2 + goal % 2))
                came.append(send(sent[(z + r) % 4], pairs))
            slot = 2 * at + core
            choice = (2 * (z % 2) + core - tiles[slot] // 2 // layers) % 4
            holds = (tiles[slot] // 2) % layers == layer
            came = jnp.where(holds, jnp.stack(came)[choice], jnp.zeros_like(came[0]))
            came = lax.psum(came, "token", axis_index_groups=layer_groups)
            queries = came if queries is None else jnp.where(layer == at, came, queries)
        queries = [queries]
        everyone = lax.all_gather(gathered, "token", axis_index_groups=group_groups)
        caches = [everyone.reshape(-1, *gathered.shape[1:])]

    guided = attend(flags, guide, queries, caches, ANY_SPEC)
    mine = [guided] + [over_z(guided, m) for m in range(1, GROUPS)]
    if layers == 1:
        others = [[over_core(piece) for piece in mine]]
    else:
        everyone = [lax.all_gather(piece, "token", axis_index_groups=group_groups) for piece in mine]
        others = [[pieces[n] for pieces in everyone] for n in range(slots)]
    return paste(flags, cached_out[0], mine, others)[None]


def solution(mesh):
    return jax.shard_map(
        body,
        mesh=mesh,
        in_specs=(
            P(None, "image", "token", None),
            P(None, "image", "token", None),
            P(None, "image", "token", None),
            P("image", "token", None),
            P("image", None),
            P("image"),
            P("image", None),
            P("image"),
        ),
        out_specs=P("image", "token", None),
        check_vma=False,
    )
```

```python
import math

import jax
import jax.numpy as jnp
from jax import lax
from jax.experimental import pallas as pl
from jax.experimental.pallas import tpu as pltpu
from jax.sharding import PartitionSpec as P

HD = 128
TILE = 128
GROUPS = 4
BF = jnp.bfloat16
F32 = jnp.float32
MIB = 1024 * 1024

SMEM_SPEC = pl.BlockSpec(memory_space=pltpu.SMEM)
ANY_SPEC = pl.BlockSpec(memory_space=pl.ANY)
VMEM_SPEC = pl.BlockSpec(memory_space=pltpu.VMEM)


def call(kernel, out_shape, scalars, arrays, scratch=(), limit=4, aliases=None, spec=ANY_SPEC, out_spec=ANY_SPEC, flops=0):
    many = isinstance(out_shape, (list, tuple))
    return pl.pallas_call(
        kernel,
        out_shape=out_shape,
        in_specs=[SMEM_SPEC] * len(scalars) + (spec if isinstance(spec, list) else [spec] * len(arrays)),
        out_specs=[out_spec] * len(out_shape) if many else out_spec,
        scratch_shapes=list(scratch),
        input_output_aliases=aliases or {},
        compiler_params=pltpu.CompilerParams(vmem_limit_bytes=limit * MIB),
        cost_estimate=pl.CostEstimate(flops=flops, bytes_accessed=0, transcendentals=0),
    )(*scalars, *arrays)


def stays(x):
    return pltpu.with_memory_space_constraint(x, pltpu.HBM)


def run_all(copies):
    for copy in copies:
        copy.start()
    for copy in copies:
        copy.wait()


def run_both(loads, stores):
    for load in loads:
        load.start()
    for load, store in zip(loads, stores):
        load.wait()
        store.start()
    for store in stores:
        store.wait()


def after(x, *events):
    def kernel(*refs):
        pass

    return call(kernel, jax.ShapeDtypeStruct(x.shape, x.dtype), [], [x, *events], aliases={0: 0})


def pack_weights(core, w_query, parts):
    rows = w_query.shape[0]
    counts = [len(heads_of(0)) for heads_of in parts]

    def kernel(core_ref, w_ref, *refs):
        outs, sem = refs[:-1], refs[-1]
        run_all(
            [
                pltpu.make_async_copy(
                    w_ref.at[:, pl.ds(pl.multiple_of(head * HD, HD), HD)],
                    outs[k].at[:, n * HD : (n + 1) * HD],
                    sem.at[sum(counts[:k]) + n],
                )
                for k, heads_of in enumerate(parts)
                for n, head in enumerate(heads_of(core_ref[0]))
            ]
        )

    return call(
        kernel,
        [jax.ShapeDtypeStruct((rows, count * HD), BF) for count in counts],
        [core],
        [stays(w_query)],
        [pltpu.SemaphoreType.DMA((sum(counts),))],
        out_spec=VMEM_SPEC,
    )


def pack_caches(key_block, value_block, events=()):
    branches, tokens, columns = key_block.shape
    width = columns // GROUPS

    def kernel(k_ref, v_ref, *refs):
        out, buf, sem, out_sem = refs[-4:]
        loads, stores = [], []
        for n, ref in enumerate((k_ref, v_ref)):
            for g in range(GROUPS):
                here = buf.at[g, n]
                loads.append(
                    pltpu.make_async_copy(
                        ref.at[:, :, g * width : (g + 1) * width], here, sem.at[n * GROUPS + g]
                    )
                )
                stores.append(pltpu.make_async_copy(here, out.at[g, n], out_sem.at[n * GROUPS + g]))
        run_both(loads, stores)

    shape = (GROUPS, 2, branches, tokens, width)
    return call(
        kernel,
        jax.ShapeDtypeStruct(shape, BF),
        [],
        [stays(key_block), stays(value_block), *events],
        [pltpu.VMEM(shape, BF), pltpu.SemaphoreType.DMA((2 * GROUPS,)), pltpu.SemaphoreType.DMA((2 * GROUPS,))],
    )


def halves(flags, guide, by_x, by_y, events=()):
    rows, width = by_x.shape
    half = rows // 2

    def kernel(_, __, x_ref, y_ref, *refs):
        first, last, sem = refs[-3:]
        run_all(
            [
                pltpu.make_async_copy(x_ref.at[:half], first, sem.at[0]),
                pltpu.make_async_copy(y_ref.at[half:], last, sem.at[1]),
            ]
        )

    return call(
        kernel,
        [jax.ShapeDtypeStruct((half, width), BF)] * 2,
        [flags, guide],
        [by_x, by_y, *events],
        [pltpu.SemaphoreType.DMA((2,))],
        out_spec=VMEM_SPEC,
    )


def begin_project(flags, at, core_at, own, other, w_query, heads_of, pieces, far_rows, events=()):
    branches, rows, depth = own.shape
    chunk, width = pieces[0].shape
    count = 1 + len(pieces)
    both = branches * rows

    def kernel(s_ref, own_ref, other_ref, w_ref, *refs):
        t_ref, far_ref, h_buf, w_buf, sem, w_sem = refs[-6:]
        loads = []
        for n in range(count + 1):
            columns = pl.ds(pl.multiple_of((s_ref[0] ^ n) * chunk, HD), chunk)
            loads.append([])
            if n == 0:
                for k, head in enumerate(heads_of(s_ref[core_at])):
                    columns_of = pl.ds(pl.multiple_of(head * HD, HD), HD)
                    loads[n].append(
                        pltpu.make_async_copy(
                            w_ref.at[:, columns_of], w_buf.at[n, :, k * HD : (k + 1) * HD], w_sem.at[k]
                        )
                    )
                    loads[n][k].start()
            elif n < count:
                loads[n].append(pltpu.make_async_copy(refs[n - 1], w_buf.at[n], w_sem.at[width // HD + n]))
                loads[n][0].start()
            for slot in range(2):
                for b in range(branches):
                    there = h_buf.at[n, slot] if n < count else far_ref.at[slot]
                    there = there.at[b * rows : (b + 1) * rows]
                    mine, theirs = [
                        pltpu.make_async_copy(ref.at[b, :, columns], there, sem.at[n, slot, b])
                        for ref in (own_ref, other_ref)
                    ]
                    loads[n].append(mine)

                    @pl.when(s_ref[at + slot] == 1)
                    def _():
                        mine.start()

                    @pl.when(s_ref[at + slot] != 1)
                    def _():
                        theirs.start()

        for n in range(count):
            for load in loads[n]:
                load.wait()
            for slot in range(2):
                product = jnp.dot(h_buf[n, slot], w_buf[n], preferred_element_type=F32)
                if n == 0:
                    t_ref[slot] = product
                else:
                    t_ref[slot] += product
        for load in loads[count]:
            load.wait()

    return call(
        kernel,
        [jax.ShapeDtypeStruct((2, both, width), F32), jax.ShapeDtypeStruct((2, both, far_rows), BF)],
        [flags],
        [own, other, stays(w_query), *pieces, *events],
        [
            pltpu.VMEM((count, 2, both, chunk), BF),
            pltpu.VMEM((count, chunk, width), BF),
            pltpu.SemaphoreType.DMA((count + 1, 2, branches)),
            pltpu.SemaphoreType.DMA((width // HD + count,)),
        ],
        limit=16,
        out_spec=VMEM_SPEC,
        flops=25_000_000_000,
    )


def finish_project(flags, first_at, sums, rows_far, pieces, earlier=(), events=()):
    _, both, width = sums.shape
    part = width // 2
    count, kept = len(pieces), len(earlier)
    before = earlier[0].shape[1] if earlier else 0

    def kernel(s_ref, t_ref, far_ref, *refs):
        w_refs, e_refs, out_refs = refs[:count], refs[count : count + kept], refs[-4:]

        def make(n, slot):
            total, first = t_ref[slot], 0
            for w_ref in w_refs:
                size = w_ref.shape[0]
                total = total + jnp.dot(
                    far_ref[slot, :, first : first + size], w_ref[...], preferred_element_type=F32
                )
                first += size
            total = total.astype(BF)
            for hi in range(2):
                out = out_refs[n * 2 + hi]
                out[:, before:] = total[:, hi * part : (hi + 1) * part]
                if e_refs:
                    out[:, :before] = e_refs[n * 2 + hi][...]

        make(0, s_ref[first_at])

        @pl.when(s_ref[first_at + 3] == 1)
        def _():
            make(1, 1)

    return call(
        kernel,
        [jax.ShapeDtypeStruct((both, before + part), BF)] * 4,
        [flags],
        [sums, rows_far, *pieces, *earlier, *events],
        limit=8,
        spec=[VMEM_SPEC] * (2 + count + kept) + [ANY_SPEC] * len(events),
        out_spec=VMEM_SPEC,
    )


def attend(flags, guide, queries, caches, q_spec=VMEM_SPEC):
    count, kept = len(queries), len(caches)
    rows, width = queries[0].shape[0] // 2, queries[0].shape[1]
    heads = width // HD
    scale = 1.0 / math.sqrt(HD)
    sizes = [c.shape[0] * c.shape[3] for c in caches]
    firsts = [sum(sizes[:i]) for i in range(kept)]
    keys_all = sum(sizes)
    step = 32 * 1024 // keys_all
    places = [(b, head) for b in range(2) for head in range(heads // 2 * 2)]
    places += [(b, head) for head in range(heads // 2 * 2, heads) for b in range(2)]
    assert heads == 3

    def kernel(s_ref, g_ref, *refs):
        q_refs, c_refs = refs[:count], refs[count : count + kept]
        out, q_buf, two_buf, s_buf, w_buf, sem = refs[-6:]
        for r in range(count):

            @pl.when(s_ref[2] == r)
            def _():
                if q_spec is VMEM_SPEC:
                    q_buf[...] = q_refs[r][...]
                else:
                    pltpu.make_async_copy(q_refs[r], q_buf, sem).start()

        for b, head in places[2 * (heads // 2 * 2) :]:
            for c_ref, size, first in zip(c_refs, sizes, firsts):
                for kind in range(2):
                    two_buf[kind, first : first + size, b * HD : (b + 1) * HD] = c_ref[
                        :, kind, b, :, head * HD : (head + 1) * HD
                    ].reshape(size, HD)
        if q_spec is not VMEM_SPEC:
            pltpu.make_async_copy(q_refs[0], q_buf, sem).wait()
        attended = {}
        for n in range(0, len(places), 2):
            pair = places[n : n + 2]
            (b0, h0), (b1, h1) = pair
            turn = n // 2 % 2
            q0 = q_buf[b0 * rows : (b0 + 1) * rows, h0 * HD : (h0 + 1) * HD]
            q1 = q_buf[b1 * rows : (b1 + 1) * rows, h1 * HD : (h1 + 1) * HD]
            none = jnp.zeros_like(q0)
            q = jnp.concatenate(
                [jnp.concatenate([q0, none], axis=1), jnp.concatenate([none, q1], axis=1)], axis=0
            )

            def sides(c_ref, kind, size, first):
                if b0 == b1:
                    return c_ref[:, kind, b0, :, h0 * HD : (h1 + 1) * HD].reshape(size, 2 * HD)
                return two_buf[kind, first : first + size]

            for c_ref, size, first in zip(c_refs, sizes, firsts):
                s_buf[turn, :, first : first + size] = lax.dot_general(
                    q, sides(c_ref, 0, size, first), (((1,), (1,)), ((), ())), preferred_element_type=F32
                )
            for row in range(0, 2 * rows, step):
                here = slice(row, row + step)
                scores = s_buf[turn, here] * scale
                exps = jnp.exp(scores - jnp.max(scores, axis=-1, keepdims=True))
                over = 1.0 / jnp.sum(exps, axis=-1, keepdims=True)
                w_buf[turn, here] = (exps * over).astype(BF)
            result = jnp.zeros((2 * rows, 2 * HD), F32)
            for c_ref, size, first in zip(c_refs, sizes, firsts):
                result = result + jnp.dot(
                    w_buf[turn, :, first : first + size],
                    sides(c_ref, 1, size, first),
                    preferred_element_type=F32,
                )
            attended[pair[0]] = result[:rows, :HD]
            attended[pair[1]] = result[rows:, HD:]
        for head in range(heads):
            guided = attended[1, head] + g_ref[0] * (attended[0, head] - attended[1, head])
            out[:, head * HD : (head + 1) * HD] = guided.astype(BF)

    return call(
        kernel,
        jax.ShapeDtypeStruct((rows, width), BF),
        [flags, guide],
        [*queries, *caches],
        [
            pltpu.VMEM((2 * rows, width), BF),
            pltpu.VMEM((2, keys_all, 2 * HD), BF),
            pltpu.VMEM((2, 2 * rows, keys_all), F32),
            pltpu.VMEM((2, 2 * rows, keys_all), BF),
            pltpu.SemaphoreType.DMA,
        ],
        limit=6 + 8 * (keys_all // 1024),
        spec=[q_spec] * count + [VMEM_SPEC] * kept,
        out_spec=VMEM_SPEC,
    )


def paste(flags, previous, mine, others):
    rows, columns = previous.shape
    width = columns // GROUPS

    def kernel(s_ref, prev_ref, *refs):
        out, sem = refs[-2:]

        def place(m):
            return out.at[:, pl.ds(pl.multiple_of((s_ref[1] ^ m) * width, HD), width)]

        taken = s_ref[3]
        for n in range(len(others)):
            taken = taken + s_ref[4 + n]

        @pl.when(taken == 0)
        def _():
            run_all([pltpu.make_async_copy(prev_ref, out, sem.at[0])])

        @pl.when(s_ref[3] == 1)
        def _():
            run_all([pltpu.make_async_copy(refs[m], place(m), sem.at[m]) for m in range(GROUPS)])

        for n in range(len(others)):

            @pl.when(s_ref[4 + n] == 1)
            def _():
                run_all(
                    [
                        pltpu.make_async_copy(refs[GROUPS * (1 + n) + m], place(m), sem.at[m])
                        for m in range(GROUPS)
                    ]
                )

    return call(
        kernel,
        jax.ShapeDtypeStruct((rows, columns), BF),
        [flags],
        [previous, *mine, *[piece for other in others for piece in other]],
        [pltpu.SemaphoreType.DMA((GROUPS,))],
        spec=VMEM_SPEC,
    )


def body(hidden, key_cache, value_cache, cached_out, w_query, guide, masked_tiles, mask_count):
    images = lax.axis_size("image")
    tokens = lax.axis_size("token")
    heads = key_cache.shape[3] // HD
    per_group = heads // GROUPS
    slots = masked_tiles.shape[1]
    layers = tokens // (2 * GROUPS)
    assert images == 4 and hidden.shape[1] == 1 and hidden.shape[2] == TILE
    assert tokens == layers * 2 * GROUPS and slots == 2 * layers and heads == per_group * GROUPS

    image = lax.axis_index("image")
    token = lax.axis_index("token")
    core = token % 2
    chip = token // 2
    z = chip // layers
    layer = chip % layers
    tiles = masked_tiles[0]

    def over_image(x, m):
        return lax.ppermute(x, "image", [(i, i ^ m) for i in range(images)])

    def over_z(x, m):
        span = 2 * layers
        return lax.ppermute(x, "token", [(t, ((t // span) ^ m) * span + t % span) for t in range(tokens)])

    def over_core(x):
        return lax.ppermute(x, "token", [(t, t ^ 1) for t in range(tokens)])

    def send(x, pairs):
        return lax.ppermute(x, "token", pairs)

    layer_groups = [
        [(s * layers + at) * 2 + c for at in range(layers)] for s in range(GROUPS) for c in range(2)
    ]
    group_groups = [list(range(s * layers * 2, (s + 1) * layers * 2)) for s in range(GROUPS)]
    z_groups = [[s * 2 * layers + at for s in range(GROUPS)] for at in range(2 * layers)]

    plan = [list(range(per_group - 1)), [per_group - 1]]

    def part_heads(k):
        return lambda c: [(2 * c + hi) * per_group + head for hi in range(2) for head in plan[k]]

    half = w_query.shape[0] // 2
    own_hidden = hidden[:, 0]
    other_hidden = over_core(own_hidden)

    in_use = jnp.arange(slots, dtype=jnp.int32) < mask_count[0]
    hit = ((tiles == token) & in_use).astype(jnp.int32)
    my_slot = layer * 2 + core
    other_hits = hit[1 - core][None] if layers == 1 else jnp.where(jnp.arange(slots) == my_slot, 0, hit)
    is_own = (tiles % 2 == core).astype(jnp.int32)
    if layers == 1:
        owners = [tiles[0] // 2, tiles[1] // 2]
        second = jnp.where(mask_count[0] > 1, owners[1], jnp.where(owners[0] < GROUPS // 2, GROUPS - 1, 0))
        which = owners[0] * GROUPS + second
        slot_first = (z != owners[0]).astype(jnp.int32)
        choice = z % 2
        shared = owners[0] == second
        extra = jnp.stack([slot_first, which, core, shared]).astype(jnp.int32)
    else:
        choice = 0
        extra = jnp.stack([0, 0, core, 1]).astype(jnp.int32)
    flags = jnp.concatenate(
        [jnp.stack([image, z, choice, hit[my_slot]]).astype(jnp.int32), other_hits, is_own, extra]
    )
    pairs_from = 4 + other_hits.shape[0]
    first_at = pairs_from + slots

    packed = pack_weights(core[None], w_query, [part_heads(k) for k in range(2)])

    def near(k):
        return [packed[k], over_image(packed[k], 1), over_image(packed[k], 2)]

    def far(k, *events):
        first, last = halves(flags, guide, weights[k][1], weights[k][2], events)
        return [over_image(first, 2), over_image(last, 1)], first

    def begin(k, *events):
        return [
            begin_project(
                flags,
                pairs_from + 2 * at,
                first_at + 2,
                own_hidden,
                other_hidden,
                w_query,
                part_heads(k),
                weights[k][1:],
                w_query.shape[0],
                events,
            )
            for at in range(layers)
        ]

    def finish(at, *events):
        first = finish_project(flags, first_at, *begun_0[at], far_0, events=events)
        return finish_project(flags, first_at, *begun_1[at], far_1, first)

    weights = [near(0)]
    blocks = pack_caches(key_cache[:, 0], value_cache[:, 0], weights[0][:1])
    gathered = lax.all_to_all(blocks, "token", 0, 0, axis_index_groups=z_groups)
    weights.append(near(1))
    far_0, event = far(0, blocks)
    begun_0 = begin(0, event)
    far_1, event = far(1, begun_0[0][1])
    begun_1 = begin(1, event)

    if layers == 1:
        sent = finish(0, begun_1[0][1])
        gathered = after(gathered, sent[0])
        caches = [gathered, over_core(gathered)]

        def ask(first, second):
            def spread(x, hi, chips):
                return send(
                    x, [(2 * chips[slot] + c, 2 * (2 * c + hi) + slot) for slot in range(2) for c in range(2)]
                )

            def branch(sent):
                if first != second:
                    return [spread(sent[hi], hi, (first, second)) for hi in range(2)]
                far_end = GROUPS - 1 if first < GROUPS // 2 else 0
                for_first = [spread(sent[hi], hi, (first, far_end)) for hi in range(2)]
                for_second = [spread(sent[2 + hi], hi, (far_end, first)) for hi in range(2)]
                return [jnp.where(core == 0, a, b) for a, b in zip(for_first, for_second)]

            return branch

        branches = [ask(a, b) for a in range(GROUPS) for b in range(GROUPS)]
        queries = lax.switch(which, branches, sent)
    else:
        queries = None
        for at in range(layers):
            sent = finish(at, begun_1[at][1])
            sent = jnp.stack([sent[0], sent[2], sent[1], sent[3]])
            came = []
            for r in range(4):
                pairs = []
                for t in range(tokens):
                    c, here, s = t % 2, (t // 2) % layers, t // 2 // layers
                    goal = (s + r) % 4
                    pairs.append((t, ((2 * c + goal // 2) * layers + here) * 2 + goal % 2))
                came.append(send(sent[(z + r) % 4], pairs))
            slot = 2 * at + core
            choice = (2 * (z % 2) + core - tiles[slot] // 2 // layers) % 4
            holds = (tiles[slot] // 2) % layers == layer
            came = jnp.where(holds, jnp.stack(came)[choice], jnp.zeros_like(came[0]))
            came = lax.psum(came, "token", axis_index_groups=layer_groups)
            queries = came if queries is None else jnp.where(layer == at, came, queries)
        queries = [queries]
        everyone = lax.all_gather(gathered, "token", axis_index_groups=group_groups)
        caches = [everyone.reshape(-1, *gathered.shape[1:])]

    guided = attend(flags, guide, queries, caches, ANY_SPEC)
    mine = [guided] + [over_z(guided, m) for m in range(1, GROUPS)]
    if layers == 1:
        others = [[over_core(piece) for piece in mine]]
    else:
        everyone = [lax.all_gather(piece, "token", axis_index_groups=group_groups) for piece in mine]
        others = [[pieces[n] for pieces in everyone] for n in range(slots)]
    return paste(flags, cached_out[0], mine, others)[None]


def solution(mesh):
    return jax.shard_map(
        body,
        mesh=mesh,
        in_specs=(
            P(None, "image", "token", None),
            P(None, "image", "token", None),
            P(None, "image", "token", None),
            P("image", "token", None),
            P("image", None),
            P("image"),
            P("image", None),
            P("image"),
        ),
        out_specs=P("image", "token", None),
        check_vma=False,
    )
```
